32 devices in a mesh: lon: 8 (over y, x, core), lat: 4 (over z).
Axes of the slice: x: 2, y: 2, z: 4, core: 2. Of those that a mesh axis runs over, the one named last changes fastest.
Arguments:
- heat_content_field: float32 [12, 384, 1024], P(None, 'lat', 'lon'), may hold values from -6 to 6
- saltiness_field: float32 [12, 384, 1024], P(None, 'lat', 'lon'), may hold values from -6 to 6
- eastward_cfl_number: float32 [12, 384, 1024], P(None, 'lat', 'lon'), may hold values from -0.4 to 0.4
- northward_cfl_number: float32 [12, 384, 1024], P(None, 'lat', 'lon'), may hold values from -0.4 to 0.4
- seawater_indicator: int32 [384, 1024], P('lat', 'lon'), may hold values 0 or 1
- submerged_layer_total: int32 [384, 1024], P('lat', 'lon'), may hold values from 1 to 12
- seam_partner_index: int32 [1024], replicated, may hold values from 0 to 1023, as said below
Outputs:
- new_temperature: float32 [12, 384, 1024], P(None, 'lat', 'lon')
- new_salinity: float32 [12, 384, 1024], P(None, 'lat', 'lon')
The draws below stay inside these ranges and needn't reach their ends.
Inputs may be any that keep to these rules, and one draw needn't show every extreme that they name: Each column appears once; the map is a reflection of the columns about a pivot, seam_partner_index[i] = (s - i) mod 1024.
All inputs are finite; a program needn't handle non-finite values. No bound on the sum of `seawater_indicator` on one device may be relied on, other than what follows from the above.
Results may differ from the reference program's by a relative error of at most 0.0003.
Values sent between devices are 32-bit elements; how exact they have to be, the bound alone decides.
No kernel may reach another device: no remote copies, remote signals or barrier semaphores. Data moves between devices by JAX's collectives and lax.ppermute only.
A program may use at most 192 MiB of HBM per device.

```python
from functools import reduce
import jax
import jax.numpy as jnp

VERTICAL_LAYERS = 12
MERIDIAN_LINES = 1024
PARALLEL_ROWS = 384


def draw_seam_partner_index(key, part):
    pivot = jax.random.randint(key, (), 0, MERIDIAN_LINES, dtype=jnp.int32)
    return ((pivot - jnp.arange(MERIDIAN_LINES, dtype=jnp.int32)) % MERIDIAN_LINES).astype(jnp.int32)


def plant(result, own_key, smallest, high):
    shape = result.shape
    place = [jax.random.randint(jax.random.fold_in(own_key, axis), (), 0, shape[axis]) for axis in range(len(shape))]
    result = result.at[tuple(place)].set(smallest)
    longest = shape.index(max(shape))
    place[longest] = (place[longest] + 1) % shape[longest]
    return result.at[tuple(place)].set(high)


def shard_levels(stream_key, extent, shards, least, high):
    loudness = 1.0
    for position, blocks in shards:
        heights = jax.random.uniform(jax.random.fold_in(jax.random.fold_in(stream_key, 6), position), (blocks,), jnp.float32, least / len(shards), high / len(shards))
        loudness = loudness * jnp.repeat(jnp.exp(heights), extent[position] // blocks).reshape((-1,) + (1,) * (len(extent) - 1 - position))
    return loudness


def bell_draw(rng, dims, deviation, most, split=(), kind=jnp.bfloat16):
    values = jax.random.normal(rng, dims, jnp.float32) * deviation
    if len(split) > 0:
        values = shard_levels(rng, dims, split, -0.22, 0.18) * values
    return jnp.clip(values, min=-most, max=most).astype(kind)


def setup_inputs(seed: int = 0) -> dict:
    splits = jax.random.split(jax.random.key(seed), 8)
    heat_content_field = bell_draw(splits[0], (VERTICAL_LAYERS, PARALLEL_ROWS, MERIDIAN_LINES), 1.0, 6.0, ((1, 4), (2, 8)), jnp.float32)
    saltiness_field = bell_draw(splits[1], (VERTICAL_LAYERS, PARALLEL_ROWS, MERIDIAN_LINES), 1.0, 6.0, ((1, 4), (2, 8)), jnp.float32)
    eastward_cfl_number = jnp.clip(jax.random.uniform(splits[2], (VERTICAL_LAYERS, PARALLEL_ROWS, MERIDIAN_LINES), jnp.float32, -0.4, 0.4) * shard_levels(splits[2], (VERTICAL_LAYERS, PARALLEL_ROWS, MERIDIAN_LINES), ((1, 4), (2, 8)), -0.4, 0.0), -0.4, 0.4)
    northward_cfl_number = jnp.clip(jax.random.uniform(splits[3], (VERTICAL_LAYERS, PARALLEL_ROWS, MERIDIAN_LINES), jnp.float32, -0.4, 0.4) * shard_levels(splits[3], (VERTICAL_LAYERS, PARALLEL_ROWS, MERIDIAN_LINES), ((1, 4), (2, 8)), -0.4, 0.0), -0.4, 0.4)
    seawater_indicator = plant((jax.random.randint(splits[4], (PARALLEL_ROWS, MERIDIAN_LINES), 0, 5) < 4).astype(jnp.int32), jax.random.fold_in(splits[4], 1), 0, 1)
    submerged_layer_total = plant(jax.random.randint(splits[5], (PARALLEL_ROWS, MERIDIAN_LINES), 1, VERTICAL_LAYERS + 1), jax.random.fold_in(splits[5], 1), 1, VERTICAL_LAYERS).astype(jnp.int32)
    seam_partner_index = draw_seam_partner_index(jax.random.fold_in(splits[7], 71), 0)
    return dict(heat_content_field=heat_content_field, saltiness_field=saltiness_field, eastward_cfl_number=eastward_cfl_number, northward_cfl_number=northward_cfl_number, seawater_indicator=seawater_indicator, submerged_layer_total=submerged_layer_total, seam_partner_index=seam_partner_index)


RATIO_FLOOR = 0.05
SLOPE_FLOOR = 0.5
SLOPE_LIMIT = 2.0
DIFFUSIVITY = 0.1
THERMAL_COEF = 0.2
HALINE_COEF = 0.8
STATE_SIGNS = (1.0, 1.0, -1.0, -1.0, 1.0)


def sign_column(values):
    return jnp.array(values, jnp.float32).reshape(len(values), 1, 1, 1)


def neighbours(field):
    at_centre = field[..., 1:-1, 1:-1]
    at_east = field[..., 1:-1, 2:]
    at_west = field[..., 1:-1, :-2]
    at_north = field[..., 2:, 1:-1]
    at_south = field[..., :-2, 1:-1]
    return at_centre, at_east, at_west, at_north, at_south


def low_order(tracer, zonal, meridional, wet_pad):
    value_centre, value_east, value_west, value_north, value_south = neighbours(tracer)
    speed_centre, _, speed_west, _, _ = neighbours(zonal)
    flow_centre, _, _, _, flow_south = neighbours(meridional)
    wet_centre, wet_east, wet_west, wet_north, wet_south = neighbours(wet_pad)
    face_east = wet_centre * wet_east
    face_west = wet_west * wet_centre
    face_north = wet_centre * wet_north
    face_south = wet_south * wet_centre
    upwind_east = face_east * (jnp.maximum(speed_centre, 0.0) * value_centre + jnp.minimum(speed_centre, 0.0) * value_east)
    upwind_west = face_west * (jnp.maximum(speed_west, 0.0) * value_west + jnp.minimum(speed_west, 0.0) * value_centre)
    upwind_north = face_north * (jnp.maximum(flow_centre, 0.0) * value_centre + jnp.minimum(flow_centre, 0.0) * value_north)
    upwind_south = face_south * (jnp.maximum(flow_south, 0.0) * value_south + jnp.minimum(flow_south, 0.0) * value_centre)
    anti_east = face_east * speed_centre * (value_centre + value_east) * 0.5 - upwind_east
    anti_west = face_west * speed_west * (value_west + value_centre) * 0.5 - upwind_west
    anti_north = face_north * flow_centre * (value_centre + value_north) * 0.5 - upwind_north
    anti_south = face_south * flow_south * (value_south + value_centre) * 0.5 - upwind_south
    upwind = value_centre - wet_centre * (upwind_east - upwind_west + upwind_north - upwind_south)
    inflow = jnp.maximum(anti_west, 0.0) - jnp.minimum(anti_east, 0.0) + jnp.maximum(anti_south, 0.0) - jnp.minimum(anti_north, 0.0)
    outflow = jnp.maximum(anti_east, 0.0) - jnp.minimum(anti_west, 0.0) + jnp.maximum(anti_north, 0.0) - jnp.minimum(anti_south, 0.0)
    anti = jnp.stack([anti_east, anti_west, anti_north, anti_south])
    return upwind, anti, inflow, outflow


def ratios(upwind_pad, wet_pad, inflow, outflow):
    value_centre, value_east, value_west, value_north, value_south = neighbours(upwind_pad)
    _, wet_east, wet_west, wet_north, wet_south = neighbours(wet_pad)
    pairs = ((value_east, wet_east), (value_west, wet_west), (value_north, wet_north), (value_south, wet_south))
    candidates = [value_centre] + [jnp.where(beside_wet > 0.5, beside, value_centre) for beside, beside_wet in pairs]
    highest = reduce(jnp.maximum, candidates)
    lowest = reduce(jnp.minimum, candidates)
    ratio_plus = jnp.minimum(1.0, (highest - value_centre) / jnp.maximum(inflow, RATIO_FLOOR))
    ratio_minus = jnp.minimum(1.0, (value_centre - lowest) / jnp.maximum(outflow, RATIO_FLOOR))
    return jnp.concatenate([ratio_plus, ratio_minus], axis=0)


def limited(ratio_pad, upwind, anti, submerged_indicator):
    plus_centre, plus_east, plus_west, plus_north, plus_south = neighbours(ratio_pad[:2])
    minus_centre, minus_east, minus_west, minus_north, minus_south = neighbours(ratio_pad[2:])
    anti_east, anti_west, anti_north, anti_south = anti[0], anti[1], anti[2], anti[3]
    coef_east = jnp.where(anti_east >= 0.0, jnp.minimum(plus_east, minus_centre), jnp.minimum(plus_centre, minus_east))
    coef_west = jnp.where(anti_west >= 0.0, jnp.minimum(plus_centre, minus_west), jnp.minimum(plus_west, minus_centre))
    coef_north = jnp.where(anti_north >= 0.0, jnp.minimum(plus_north, minus_centre), jnp.minimum(plus_centre, minus_north))
    coef_south = jnp.where(anti_south >= 0.0, jnp.minimum(plus_centre, minus_south), jnp.minimum(plus_south, minus_centre))
    return upwind - submerged_indicator * (coef_east * anti_east - coef_west * anti_west + coef_north * anti_north - coef_south * anti_south)


def isopycnal(tracer_pad, wet_pad):
    stacked_wet = wet_pad[:-1] * wet_pad[1:]
    vertical = (tracer_pad[:, 1:] - tracer_pad[:, :-1]) * stacked_wet
    vertical = jnp.concatenate([vertical, jnp.zeros_like(tracer_pad[:, :1])], axis=1)
    density = HALINE_COEF * tracer_pad[1] - THERMAL_COEF * tracer_pad[0]
    stratification = HALINE_COEF * vertical[1] - THERMAL_COEF * vertical[0]
    values = neighbours(tracer_pad)
    verticals = neighbours(vertical)
    densities = neighbours(density)
    stratas = neighbours(stratification)
    wet_sides = neighbours(wet_pad)

    def face_flux(first, second):
        face = wet_sides[first] * wet_sides[second]
        slope = jnp.clip((densities[second] - densities[first]) / jnp.maximum(0.5 * (stratas[first] + stratas[second]), SLOPE_FLOOR), -SLOPE_LIMIT, SLOPE_LIMIT)
        return DIFFUSIVITY * face * ((values[second] - values[first]) - slope * 0.5 * (verticals[first] + verticals[second]))

    east_flux = face_flux(0, 1)
    west_flux = face_flux(2, 0)
    north_flux = face_flux(0, 3)
    south_flux = face_flux(4, 0)
    return values[0] + wet_sides[0] * (east_flux - west_flux + north_flux - south_flux)


def extend(field, signs, seam_partner_index):
    ghost = jnp.take(field[:, :, -1:, :], seam_partner_index, axis=3) * signs
    bottom = jnp.zeros_like(ghost)
    tall = jnp.concatenate([bottom, field, ghost], axis=2)
    return jnp.concatenate([tall[..., -1:], tall, tall[..., :1]], axis=3)


def reference(heat_content_field, saltiness_field, eastward_cfl_number, northward_cfl_number, seawater_indicator, submerged_layer_total, seam_partner_index):
    vertical_layer = jnp.arange(VERTICAL_LAYERS, dtype=jnp.int32)[:, None, None]
    submerged_indicator = ((seawater_indicator[None] == 1) & (vertical_layer < submerged_layer_total[None])).astype(jnp.float32)
    scalar_fields_pair = jnp.stack([heat_content_field, saltiness_field, eastward_cfl_number, northward_cfl_number, submerged_indicator])
    padded = extend(scalar_fields_pair, sign_column(STATE_SIGNS), seam_partner_index)
    upwind, anti, inflow, outflow = low_order(padded[:2], padded[2], padded[3], padded[4])
    ratio = ratios(extend(upwind, sign_column((1.0, 1.0)), seam_partner_index), padded[4], inflow, outflow)
    advected = limited(extend(ratio, sign_column((1.0, 1.0, 1.0, 1.0)), seam_partner_index), upwind, anti, submerged_indicator)
    final = isopycnal(extend(advected, sign_column((1.0, 1.0)), seam_partner_index), padded[4])
    return final[0], final[1]
```

```python
import functools

import jax
import jax.numpy as jnp
from jax import lax
from jax.experimental import pallas as pl
from jax.experimental.pallas import tpu as pltpu
from jax.sharding import PartitionSpec as P

RATIO_FLOOR = 0.05
DIFFUSIVITY = 0.1
THERMAL_COEF = 0.2
HALINE_COEF = 0.8

HALO = 4
SUB = 8
LANES = 128
VMEM_BYTES = 56 * 1024 * 1024


def sublanes():
    return lax.broadcasted_iota(jnp.int32, (SUB, LANES), 0)


def lanes():
    return lax.broadcasted_iota(jnp.int32, (SUB, LANES), 1)


def half_turn(tile):
    return pltpu.roll(tile, 4, 0)


def as_mask(flag):
    return (jnp.zeros((SUB, LANES), jnp.int32) + flag) > 0


def wet_count(indicator, total):
    return jnp.where(indicator == 1, total, 0).astype(jnp.float32)


def pack_rows(levels, *refs):
    south, north, (ind_s, ind_n, tot_s, tot_n), (first, second) = refs[:4], refs[4:8], refs[8:12], refs[12:]
    lat = lax.axis_index("lat")
    odd = as_mask(lat % 2)
    upper = sublanes() >= HALO
    for i in range(2 * levels):
        f, k = divmod(i, levels)
        low = jnp.where(upper, half_turn(south[f + 2][k]), south[f][k])
        high = jnp.where(upper, north[f][k], half_turn(north[f + 2][k]))
        first[i] = jnp.where(odd, low, high)
        second[i] = jnp.where(odd, high, low)
    low = wet_count(ind_s[...], tot_s[...])
    high = wet_count(ind_n[...], tot_n[...])
    first[2 * levels] = jnp.where(odd, low, high)
    second[2 * levels] = jnp.where(odd, high, low)

    @pl.when(lat == lax.axis_size("lat") - 1)
    def _():
        for i in range(2 * levels):
            f, k = divmod(i, levels)
            for j in range(HALO):
                second[i, j : j + 1, :] = north[f][k, 7 - j : 8 - j, :]
                row = 7 - j if f == 0 else (6, 5, 4, 7)[j]
                second[i, HALO + j : HALO + j + 1, :] = -north[f + 2][k, row : row + 1, :]
        for j in range(HALO):
            second[2 * levels, j : j + 1, :] = wet_count(ind_n[7 - j : 8 - j, :], tot_n[7 - j : 8 - j, :])


def pack_columns(levels, tiles, *refs):
    fields, ind, tot, q1, q2, own, to_east, to_west = refs[:4], *refs[4:]
    odd = as_mask(lax.axis_index("lat") % 2)
    lane = lanes()
    upper = sublanes() >= HALO
    count = 4 * levels + 1
    half = 2 * levels

    def halo_tile(fl):
        i = fl % half
        one, two = q1[2 * levels if fl == 2 * half else i], q2[2 * levels if fl == 2 * half else i]
        north, south = jnp.where(odd, two, one), jnp.where(odd, one, two)
        if half <= fl < 2 * half:
            return half_turn(jnp.where(upper, north, south))
        return jnp.where(upper, south, north)

    def piece(fl, t):
        if t >= tiles:
            return halo_tile(fl)
        rows = pl.ds(t * SUB, SUB)
        if fl == 2 * half:
            return wet_count(ind[rows, :], tot[rows, :])
        f, k = divmod(fl, levels)
        return fields[f][k, rows, :]

    for g in range(0, count, 8):
        members = range(g, min(g + 8, count))
        column = []
        for t in range(tiles + 1):
            tile = None
            for j, fl in enumerate(members):
                moved = pltpu.roll(piece(fl, t), (16 * j + 8) % LANES, 1)
                tile = moved if tile is None else jnp.where(lane >= 16 * j, moved, tile)
            column.append(tile)
        while len(column) < LANES // SUB:
            column.append(column[tiles])
        turned = jnp.concatenate(column, axis=0).T
        for j, fl in enumerate(members):
            own[fl] = turned[16 * j : 16 * j + 16]
    for i in range(half):
        to_east[i] = jnp.where(upper, own[i, 0:8, :], half_turn(own[i + half, 0:8, :]))
        to_west[i] = jnp.where(upper, half_turn(own[i + half, 8:16, :]), own[i, 8:16, :])
    to_east[half] = own[2 * half, 0:8, :]
    to_west[half] = own[2 * half, 8:16, :]
    for i in range(half + 1):
        to_east[half + 1 + i] = q2[i]
        to_west[half + 1 + i] = q2[i]


def ahead(tiles):
    return tiles[1:] + [pltpu.roll(tiles[0], SUB - 1, 0)]


def behind(tiles):
    return [pltpu.roll(tiles[-1], 1, 0)] + tiles[:-1]


def right(tiles):
    return [pltpu.roll(x, LANES - 1, 1) for x in tiles]


def left(tiles):
    return [pltpu.roll(x, 1, 1) for x in tiles]


def each(function, *lists):
    return [function(*items) for items in zip(*lists)]


def replaced(tiles, other):
    return [other.get(t, x) for t, x in enumerate(tiles)]


def flux_pair(q, q_next, half_speed, half_size):
    anti = half_size * (q_next - q)
    return half_speed * (q_next + q) - anti, anti


def limited_flux(anti, plus, minus, plus_next, minus_next):
    return anti * jnp.where(anti >= 0.0, jnp.minimum(plus_next, minus), jnp.minimum(plus, minus_next))


def reciprocal(x):
    return pl.reciprocal(x, approx=True)


def advect(tracer, along, across, open_along, open_across, along_alt, across_alt):
    q_a, q_c = ahead(tracer), right(tracer)
    low_a, anti_a = map(list, zip(*each(flux_pair, tracer, q_a, *along)))
    low_c, anti_c = map(list, zip(*each(flux_pair, tracer, q_c, *across)))
    alt_a = {t: flux_pair(tracer[t], q_a[t], *v) for t, v in along_alt.items()}
    alt_c = {t: flux_pair(tracer[t], q_c[t], *v) for t, v in across_alt.items()}
    low_b = behind(replaced(low_a, {t: v[0] for t, v in alt_a.items()}))
    anti_b = behind(replaced(anti_a, {t: v[1] for t, v in alt_a.items()}))
    low_l = left(replaced(low_c, {t: v[0] for t, v in alt_c.items()}))
    anti_l = left(replaced(anti_c, {t: v[1] for t, v in alt_c.items()}))
    upwind = each(lambda q, a, b, c, d: q - ((a - b) + (c - d)), tracer, low_a, low_b, low_c, low_l)

    up_a, up_c = ahead(upwind), right(upwind)
    step_a = each(lambda u, n, m: jnp.where(m, n - u, 0.0), upwind, up_a, open_along)
    step_c = each(lambda u, n, m: jnp.where(m, n - u, 0.0), upwind, up_c, open_across)
    step_b, step_l = behind(step_a), left(step_c)

    def ratios(a, b, c, l, sa, sb, sc, sl):
        inflow = (jnp.maximum(b, 0.0) - jnp.minimum(a, 0.0)) + (jnp.maximum(l, 0.0) - jnp.minimum(c, 0.0))
        outflow = (jnp.maximum(a, 0.0) - jnp.minimum(b, 0.0)) + (jnp.maximum(c, 0.0) - jnp.minimum(l, 0.0))
        rise = jnp.maximum(jnp.maximum(jnp.maximum(sa, sc), 0.0), -jnp.minimum(sb, sl))
        drop = jnp.maximum(jnp.maximum(jnp.maximum(sb, sl), 0.0), -jnp.minimum(sa, sc))
        plus = jnp.minimum(1.0, rise * reciprocal(jnp.maximum(inflow, RATIO_FLOOR)))
        minus = jnp.minimum(1.0, drop * reciprocal(jnp.maximum(outflow, RATIO_FLOOR)))
        return plus, minus

    plus, minus = map(
        list, zip(*each(ratios, anti_a, anti_b, anti_c, anti_l, step_a, step_b, step_c, step_l))
    )
    plus_a, minus_a, plus_c, minus_c = ahead(plus), ahead(minus), right(plus), right(minus)
    lim_a = each(limited_flux, anti_a, plus, minus, plus_a, minus_a)
    lim_c = each(limited_flux, anti_c, plus, minus, plus_c, minus_c)
    lim_b = behind(
        replaced(lim_a, {t: limited_flux(v[1], plus[t], minus[t], plus_a[t], minus_a[t]) for t, v in alt_a.items()})
    )
    lim_l = left(
        replaced(lim_c, {t: limited_flux(v[1], plus[t], minus[t], plus_c[t], minus_c[t]) for t, v in alt_c.items()})
    )
    return each(lambda u, a, b, c, d: u - ((a - b) + (c - d)), upwind, lim_a, lim_b, lim_c, lim_l)


def diffuse(temp, salt, temp_below, salt_below, stacked, open_along, open_across):
    dz_t = each(lambda x, y, m: jnp.where(m, y - x, 0.0), temp, temp_below, stacked)
    dz_s = each(lambda x, y, m: jnp.where(m, y - x, 0.0), salt, salt_below, stacked)

    def face(t0, t1, s0, s1, zt0, zt1, zs0, zs1, m):
        dt, ds, zt, zs = t1 - t0, s1 - s0, zt1 + zt0, zs1 + zs0
        bottom = jnp.maximum(HALINE_COEF * zs - THERMAL_COEF * zt, 1.0)
        half_slope = (HALINE_COEF * ds - THERMAL_COEF * dt) * reciprocal(bottom)
        half_slope = jnp.maximum(jnp.minimum(half_slope, 1.0), -1.0)
        return jnp.where(m, dt - half_slope * zt, 0.0), jnp.where(m, ds - half_slope * zs, 0.0)

    def faces(shift, mask):
        parts = each(face, temp, shift(temp), salt, shift(salt), dz_t, shift(dz_t), dz_s, shift(dz_s), mask)
        return map(list, zip(*parts))

    t_a, s_a = faces(ahead, open_along)
    t_c, s_c = faces(right, open_across)

    def total(q, a, b, c, d):
        return q + DIFFUSIVITY * ((a - b) + (c - d))

    return (
        each(total, temp, t_a, behind(t_a), t_c, left(t_c)),
        each(total, salt, s_a, behind(s_a), s_c, left(s_c)),
    )


def halves(speed, mask):
    half = jnp.where(mask, 0.5 * speed, 0.0)
    return half, jnp.abs(half)


def step(levels, rows, *refs):
    (
        seam, q1, q2, from_east, from_west, own, ind, tot, temp_in, salt_in, east_in, north_in,
        temp_out, salt_out,
        pad, count, opens, strip, strip_opens, north_halo, adv, strip_adv, out, strip_out, sems,
    ) = refs
    half = 2 * levels
    flat = 4 * levels
    nt = rows // SUB + 1
    period = nt * SUB
    width = LANES
    nl = lax.axis_size("lon")
    lat = lax.axis_index("lat")
    on_top = lat == lax.axis_size("lat") - 1
    odd = as_mask(lat % 2)
    lane, sub = lanes(), sublanes()
    upper = sub >= HALO
    tops = as_mask(on_top.astype(jnp.int32))

    loads = [
        pltpu.make_async_copy(ref, pad.at[f, :, 0:rows, :], sems.at[f])
        for f, ref in enumerate((temp_in, salt_in, east_in, north_in))
    ]
    for load in loads:
        load.start()

    for i in range(half + 1):
        north_halo[i] = jnp.where(odd, q2[i], q1[i])
        if i < half:
            strip[i, 8:16, :] = jnp.where(upper, from_west[i], from_east[i])
            strip[i + half, 8:16, :] = half_turn(jnp.where(upper, from_east[i], from_west[i]))
        else:
            strip[flat, 8:16, :] = jnp.where(upper, from_west[i], from_east[i])
    for fl in range(flat + 1):
        strip[fl, 0:8, :] = own[fl, 0:8, :]
        strip[fl, 16:24, :] = own[fl, 8:16, :]

    @pl.when(on_top)
    def _():
        r = seam[0] % width
        shift = r + jnp.where(2 * r < width, width, 0)

        def facing(i, column):
            at = shift - column - jnp.where(upper, 1 if i < levels else 0, 0)
            index = at & (width - 1)

            def pick(tile):
                return jnp.take_along_axis(tile, index, axis=1, mode="promise_in_bounds")

            here = pick(q2[i])
            east = pick(from_east[half + 1 + i])
            west = pick(from_west[half + 1 + i])
            return jnp.where(at < 0, east, jnp.where(at >= width, west, here))

        edge = jnp.where(lane < 12, 120 + lane, lane - 16)
        corner = []
        for i in range(half + 1):
            north_halo[i] = facing(i, lane)
            corner.append(facing(i, edge))
        while len(corner) % 16:
            corner.append(jnp.zeros((SUB, LANES), jnp.float32))
        here = (lane >= rows) & (lane < rows + HALO)
        for g in range(0, len(corner), 16):
            turned = jnp.concatenate(corner[g : g + 16], axis=0).T
            for i in range(g, min(g + 16, half + 1)):
                for fl, at in ((i, 0), (i + half, HALO)) if i < half else ((flat, 0),):
                    for a in range(0, 24, 8):
                        moved = pltpu.roll(turned[a : a + 8], (rows - 8 * (i - g) - at) % LANES, 1)
                        strip[fl, a : a + 8, :] = jnp.where(here, moved, strip[fl, a : a + 8, :])

    for i in range(half):
        f, k = divmod(i, levels)
        n_tile, s_tile = north_halo[i], jnp.where(odd, q1[i], q2[i])
        pad[f, k, rows:period, :] = jnp.where(upper, s_tile, n_tile)
        pad[f + 2, k, rows:period, :] = half_turn(jnp.where(upper, n_tile, s_tile))
    count[0:rows, :] = wet_count(ind[...], tot[...])
    count[rows:period, :] = jnp.where(upper, jnp.where(odd, q1[half], q2[half]), north_halo[half])

    def open_counts(source, target, tiles):
        n = [source[pl.ds(t, SUB, stride=tiles), :] for t in range(tiles)]
        for t, (c, a, b) in enumerate(zip(n, ahead(n), right(n))):
            target[0, t] = c
            target[1, t] = jnp.minimum(c, a)
            target[2, t] = jnp.minimum(c, b)

    open_counts(count, opens, nt)
    open_counts(strip.at[flat], strip_opens, 3)

    def wet_faces(source, tiles, k):
        level = k.astype(jnp.float32)
        return (
            [source[1, t] > level for t in range(tiles)],
            [source[2, t] > level for t in range(tiles)],
            [source[0, t] > level + 1.0 for t in range(tiles)],
        )

    for load in loads:
        load.wait()

    seam_tile = (rows - 1) % nt
    seam_sub = (rows - 1) // nt
    spare_tile = (rows + HALO - 1) % nt

    def main_advect(k, carry):
        def tiles_of(f):
            return [pad.at[f, k][pl.ds(t, SUB, stride=nt), :] for t in range(nt)]

        along_open, across_open, _ = wet_faces(opens, nt, k)
        v = tiles_of(3)
        along = list(zip(*each(halves, v, along_open)))
        across = list(zip(*each(halves, tiles_of(2), across_open)))
        turned = jnp.where((sub == seam_sub) & tops, v[spare_tile], v[seam_tile])
        alt = {seam_tile: halves(turned, along_open[seam_tile])}
        for f in range(2):
            result = advect(tiles_of(f), along, across, along_open, across_open, alt, {})
            for t in range(nt):
                adv[f, k, t] = result[t]
        return carry

    def strip_advect(group, carry):
        for j in range(4):
            k = group * 4 + j

            def tiles_of(f):
                return [strip.at[f * levels + k][pl.ds(t, SUB, stride=3), :] for t in range(3)]

            along_open, across_open, _ = wet_faces(strip_opens, 3, k)
            v = tiles_of(3)
            along = list(zip(*each(halves, tiles_of(2), along_open)))
            across = list(zip(*each(halves, v, across_open)))
            fold = (lane == rows - 1) & tops
            alt = {
                t: halves(jnp.where(fold, pltpu.roll(x, LANES - HALO, 1), x), m)
                for t, (x, m) in enumerate(zip(v, across_open))
            }
            for f in range(2):
                result = advect(tiles_of(f), along, across, along_open, across_open, {}, alt)
                for t in range(3):
                    strip_adv[f, k, t] = result[t]
        return carry

    def diffuse_level(source, counts, tiles, k):
        below = jnp.minimum(k + 1, levels - 1)
        along_open, across_open, stacked = wet_faces(counts, tiles, k)
        fields = [[source[f, at, t] for t in range(tiles)] for at in (k, below) for f in range(2)]
        return diffuse(*fields, stacked, along_open, across_open)

    def main_diffuse(k, carry):
        for f, result in enumerate(diffuse_level(adv, opens, nt, k)):
            for t in range(nt):
                out.at[f, k][pl.ds(t, SUB, stride=nt), :] = result[t]
        return carry

    def strip_diffuse(group, carry):
        for j in range(4):
            k = group * 4 + j
            for f, result in enumerate(diffuse_level(strip_adv, strip_opens, 3, k)):
                for t in range(3):
                    strip_out.at[f * levels + k][pl.ds(t, SUB, stride=3), :] = result[t]
        return carry

    lax.fori_loop(0, levels // 4, strip_advect, 0)
    lax.fori_loop(0, levels // 4, strip_diffuse, 0)
    lax.fori_loop(0, levels, main_advect, 0)
    lax.fori_loop(0, levels, main_diffuse, 0)

    at_edge = (lane < HALO) | (lane >= LANES - HALO)
    for g in range(0, half, 8):
        column = []
        for i in range(g, g + 8):
            column += [strip_out[i, 0:8, :], strip_out[i, 16:24, :]]
        turned = jnp.concatenate(column, axis=0).T
        for i in range(g, g + 8):
            f, k = divmod(i, levels)
            back = (LANES - 16 * (i - g) - 8) % LANES
            for t in range(rows // SUB):
                moved = pltpu.roll(turned[t * SUB : t * SUB + SUB], back, 1)
                at = pl.ds(t * SUB, SUB)
                out[f, k, at, :] = jnp.where(at_edge, moved, out[f, k, at, :])
    stores = [
        pltpu.make_async_copy(out.at[f, :, 0:rows, :], ref, sems.at[f])
        for f, ref in enumerate((temp_out, salt_out))
    ]
    for store in stores:
        store.start()
    for store in stores:
        store.wait()


def local(nl, nlat, temp, salt, east, north, indicator, total, seam):
    levels, rows, width = temp.shape
    half = 2 * levels
    vmem = pl.BlockSpec(memory_space=pltpu.VMEM)
    anywhere = pl.BlockSpec(memory_space=pl.ANY)
    params = pltpu.CompilerParams(vmem_limit_bytes=VMEM_BYTES)
    f32 = jnp.float32

    last = rows // SUB - 1
    low = pl.BlockSpec((levels, SUB, width), lambda i: (0, 0, 0))
    high = pl.BlockSpec((levels, SUB, width), lambda i: (0, last, 0))
    flat_low = pl.BlockSpec((SUB, width), lambda i: (0, 0))
    flat_high = pl.BlockSpec((SUB, width), lambda i: (last, 0))
    block = jax.ShapeDtypeStruct((half + 1, SUB, width), f32)
    whole_block = pl.BlockSpec((half + 1, SUB, width), lambda i: (0, 0, 0))
    fields = (temp, salt, east, north)
    first, second = pl.pallas_call(
        functools.partial(pack_rows, levels),
        grid=(1,),
        in_specs=[low] * 4 + [high] * 4 + [flat_low, flat_high] * 2,
        out_specs=[whole_block] * 2,
        out_shape=[block] * 2,
        compiler_params=params,
    )(*fields, *fields, indicator, indicator, total, total)

    pivot = seam[0]
    low_half = 2 * (pivot % width) < width
    turn = (pivot // width - low_half.astype(jnp.int32)) % nl
    q1 = lax.ppermute(first, "lat", [(j, j ^ 1) for j in range(nlat)])

    def meet(turned):
        pairs = [(i * nlat + j, i * nlat + (j + 1 if j % 2 else j - 1)) for i in range(nl) for j in range(1, nlat - 1)]
        pairs += [(i * nlat + nlat - 1, (turned - i) % nl * nlat + nlat - 1) for i in range(nl)]
        return lambda x: lax.ppermute(x, ("lon", "lat"), pairs)

    q2 = lax.switch(turn, [meet(t) for t in range(nl)], second)

    strip_count = 2 * half + 1
    payload = jax.ShapeDtypeStruct((2 * half + 2, SUB, width), f32)
    own, to_east, to_west = pl.pallas_call(
        functools.partial(pack_columns, levels, rows // SUB),
        in_specs=[vmem] * 8,
        out_specs=[vmem] * 3,
        out_shape=[jax.ShapeDtypeStruct((strip_count, 2 * SUB, width), f32), payload, payload],
        compiler_params=params,
    )(*fields, indicator, total, q1, q2)
    from_west = lax.ppermute(to_east, "lon", [(i, (i + 1) % nl) for i in range(nl)])
    from_east = lax.ppermute(to_west, "lon", [((i + 1) % nl, i) for i in range(nl)])

    nt = rows // SUB + 1
    period = nt * SUB
    return pl.pallas_call(
        functools.partial(step, levels, rows),
        in_specs=[pl.BlockSpec(memory_space=pltpu.SMEM)] + [vmem] * 7 + [anywhere] * 4,
        out_specs=[anywhere] * 2,
        out_shape=[jax.ShapeDtypeStruct(temp.shape, f32)] * 2,
        scratch_shapes=[
            pltpu.VMEM((4, levels, period, width), f32),
            pltpu.VMEM((period, width), f32),
            pltpu.VMEM((3, nt, SUB, width), f32),
            pltpu.VMEM((strip_count, 24, width), f32),
            pltpu.VMEM((3, 3, SUB, width), f32),
            pltpu.VMEM((half + 1, SUB, width), f32),
            pltpu.VMEM((2, levels, nt, SUB, width), f32),
            pltpu.VMEM((2, levels, 3, SUB, width), f32),
            pltpu.VMEM((2, levels, period, width), f32),
            pltpu.VMEM((half, 24, width), f32),
            pltpu.SemaphoreType.DMA((4,)),
        ],
        compiler_params=params,
    )(seam, q1, q2, from_east, from_west, own, indicator, total, *fields)


def solution(mesh):
    in_specs = (
        P(None, "lat", "lon"),
        P(None, "lat", "lon"),
        P(None, "lat", "lon"),
        P(None, "lat", "lon"),
        P("lat", "lon"),
        P("lat", "lon"),
        P(),
    )
    out_specs = (P(None, "lat", "lon"), P(None, "lat", "lon"))
    body = functools.partial(local, mesh.shape["lon"], mesh.shape["lat"])
    return jax.shard_map(body, mesh=mesh, in_specs=in_specs, out_specs=out_specs, check_vma=False)
```

```python
import functools

import jax
import jax.numpy as jnp
from jax import lax
from jax.experimental import pallas as pl
from jax.experimental.pallas import tpu as pltpu
from jax.sharding import PartitionSpec as P

RATIO_FLOOR = 0.05
DIFFUSIVITY = 0.1
THERMAL_COEF = 0.2
HALINE_COEF = 0.8

UNROLL = 6
HALO = 4
SUB = 8
LANES = 128


def sublanes():
    return lax.broadcasted_iota(jnp.int32, (SUB, LANES), 0)


def lanes():
    return lax.broadcasted_iota(jnp.int32, (SUB, LANES), 1)


def half_turn(tile):
    return pltpu.roll(tile, 4, 0)


def as_mask(flag):
    return (jnp.zeros((SUB, LANES), jnp.int32) + flag) > 0


def wet_count(indicator, total):
    return jnp.where(indicator == 1, total, 0).astype(jnp.float32)


def pack_rows(levels, width, seam, *refs):
    south, north, (ind_s, ind_n, tot_s, tot_n), (first, second, turn) = refs[:4], refs[4:8], refs[8:12], refs[12:]
    turn[0] = lax.div(seam[0], width)
    lat = lax.axis_index("lat")
    odd = as_mask(lat % 2)
    upper = sublanes() >= HALO
    for i in range(2 * levels):
        f, k = divmod(i, levels)
        low = jnp.where(upper, half_turn(south[f + 2][k]), south[f][k])
        high = jnp.where(upper, north[f][k], half_turn(north[f + 2][k]))
        first[i] = jnp.where(odd, low, high)
        second[i] = jnp.where(odd, high, low)
    low = wet_count(ind_s[...], tot_s[...])
    high = wet_count(ind_n[...], tot_n[...])
    first[2 * levels] = jnp.where(odd, low, high)
    second[2 * levels] = jnp.where(odd, high, low)

    @pl.when(lat == lax.axis_size("lat") - 1)
    def _():
        for i in range(2 * levels):
            f, k = divmod(i, levels)
            for j in range(HALO):
                second[i, j : j + 1, :] = north[f][k, 7 - j : 8 - j, :]
                row = 7 - j if f == 0 else (6, 5, 4, 7)[j]
                second[i, HALO + j : HALO + j + 1, :] = -north[f + 2][k, row : row + 1, :]
        for j in range(HALO):
            second[2 * levels, j : j + 1, :] = wet_count(ind_n[7 - j : 8 - j, :], tot_n[7 - j : 8 - j, :])


def stretch(levels, rows):
    blocks = LANES // levels
    stride = -(-(rows + 2 * HALO) // blocks)
    return blocks, stride, blocks * stride, -(-(HALO + stride * LANES) // SUB) * SUB


def turn_fields(levels, rows, seam, *refs):
    fields, ind, tot, q1, q2, q3, turned, to_east, to_west, flat, north_halo, spare = refs[:4], *refs[4:]
    blocks, stride, period, length = stretch(levels, rows)
    half = 2 * levels
    lat = lax.axis_index("lat")
    odd = as_mask(lat % 2)
    lane = lanes()
    upper = sublanes() >= HALO
    zero = jnp.zeros((SUB, LANES), jnp.float32)

    for i in range(half + 1):
        north_halo[i] = jnp.where(odd, q2[i], q1[i])

    @pl.when(lat == lax.axis_size("lat") - 1)
    def _():
        r = seam[0] & (LANES - 1)
        for i in range(half + 1):
            at = r - lane - jnp.where(upper, 1 if i < levels else 0, 0)
            index = at & (LANES - 1)

            def pick(tile):
                return jnp.take_along_axis(tile, index, axis=1, mode="promise_in_bounds")

            north_halo[i] = jnp.where(at < 0, pick(q3[i]), pick(q2[i]))

    tiles = rows // SUB
    for f in range(4):

        def fill(k, carry):
            at = HALO + HALO + k * period
            for t in range(tiles):
                flat[f, pl.ds(at + t * SUB, SUB), :] = fields[f][k, t * SUB : t * SUB + SUB, :]
            i = (f % 2) * levels + k
            n_tile, s_tile = north_halo[i], jnp.where(odd, q1[i], q2[i])
            if f >= 2:
                n_tile, s_tile = half_turn(n_tile), half_turn(s_tile)
            flat[f, pl.ds(at - SUB, SUB), :] = jnp.where(upper, s_tile, 0.0)
            flat[f, pl.ds(at + rows, SUB), :] = jnp.where(upper, 0.0, n_tile)
            return carry

        lax.fori_loop(0, levels, fill, 0, unroll=4)
    for t in range(tiles + 2):
        if t == 0:
            n = jnp.where(upper, jnp.where(odd, q1[half], q2[half]), 0.0)
        elif t == tiles + 1:
            n = jnp.where(upper, 0.0, north_halo[half])
        else:
            n = wet_count(ind[t * SUB - SUB : t * SUB, :], tot[t * SUB - SUB : t * SUB, :])

        def left_over(k, carry):
            flat[4, pl.ds(HALO + HALO + k * period + (t - 1) * SUB, SUB), :] = n - k.astype(jnp.float32)
            return carry

        lax.fori_loop(0, levels, left_over, 0, unroll=4)
    end = levels * period
    for f in range(5):
        for t in range(end // SUB * SUB, length, SUB):
            keep = sublanes() + t < end
            flat[f, t : t + SUB, :] = jnp.where(keep, flat[f, t : t + SUB, :], 0.0)

    for t in range(stride):
        for f in range(5):
            turned[f, t] = flat.at[f][pl.ds(HALO + t, LANES, stride=stride), :].T

    places = [(f, t) for f in range(5) for t in range(stride)]
    first = (len(places) + 1) // 2
    for i in range(first):
        f, t = places[i]
        west, east = turned[f, t, 0:SUB, :], turned[f, t, LANES - SUB : LANES, :]
        if i + first < len(places):
            f, t = places[i + first]
            west = jnp.where(upper, half_turn(turned[f, t, 0:SUB, :]), west)
            east = jnp.where(upper, east, half_turn(turned[f, t, LANES - SUB : LANES, :]))
        to_west[i] = west
        to_east[i] = east


def ahead(tiles):
    return tiles[1:] + [pltpu.roll(tiles[0], LANES - 1, 1)]


def behind(tiles):
    return [pltpu.roll(tiles[-1], 1, 1)] + tiles[:-1]


def each(function, *lists):
    return [function(*items) for items in zip(*lists)]


def pairs(function, *lists):
    return tuple(map(list, zip(*each(function, *lists))))


def replaced(tiles, other):
    return [other.get(t, x) for t, x in enumerate(tiles)]


def flux_pair(q, q_next, half_speed, half_size):
    anti = half_size * (q_next - q)
    return half_speed * (q_next + q) - anti, anti


def limited_flux(anti, plus, minus, plus_next, minus_next):
    return anti * jnp.where(anti >= 0.0, jnp.minimum(plus_next, minus), jnp.minimum(plus, minus_next))


def reciprocal(x):
    return pl.reciprocal(x, approx=True)


def halves(speed, mask):
    half = jnp.where(mask > 0.0, 0.5 * speed, 0.0)
    return half, jnp.abs(half)


def net(q, a, b, c, d):
    return q - ((a - b) + (c - d))


def ratios(a, b, c, l, sa, sb, sc, sl):
    inflow = (jnp.maximum(b, 0.0) - jnp.minimum(a, 0.0)) + (jnp.maximum(l, 0.0) - jnp.minimum(c, 0.0))
    outflow = (jnp.maximum(a, 0.0) - jnp.minimum(b, 0.0)) + (jnp.maximum(c, 0.0) - jnp.minimum(l, 0.0))
    rise = jnp.maximum(jnp.maximum(jnp.maximum(sa, sc), 0.0), -jnp.minimum(sb, sl))
    drop = jnp.maximum(jnp.maximum(jnp.maximum(sb, sl), 0.0), -jnp.minimum(sa, sc))
    plus = jnp.minimum(1.0, rise * reciprocal(jnp.maximum(inflow, RATIO_FLOOR)))
    minus = jnp.minimum(1.0, drop * reciprocal(jnp.maximum(outflow, RATIO_FLOOR)))
    return plus, minus


def face(t0, t1, s0, s1, zt0, zt1, zs0, zs1, m):
    dt, ds, zt, zs = t1 - t0, s1 - s0, zt1 + zt0, zs1 + zs0
    bottom = jnp.maximum(HALINE_COEF * zs - THERMAL_COEF * zt, 1.0)
    half_slope = (HALINE_COEF * ds - THERMAL_COEF * dt) * reciprocal(bottom)
    half_slope = jnp.maximum(jnp.minimum(half_slope, 1.0), -1.0)
    return jnp.where(m > 0.0, dt - half_slope * zt, 0.0), jnp.where(m > 0.0, ds - half_slope * zs, 0.0)


def step(levels, rows, *refs):
    (
        turned, from_east, from_west, temp_out, salt_out,
        body, result, flat, out, sems, *grid
    ) = refs
    grid, alts, prev = grid[:17], grid[17:19], grid[19:]
    blocks, stride, period, length = stretch(levels, rows)
    columns = LANES + 2 * HALO
    nc = columns // SUB
    ts = range(stride)
    lat = lax.axis_index("lat")
    tops = as_mask((lat == lax.axis_size("lat") - 1).astype(jnp.int32))
    lane = lanes()
    upper = sublanes() >= HALO
    loads = [
        pltpu.make_async_copy(turned.at[f], body.at[f, :, 0:LANES, :], sems.at[f]) for f in range(5)
    ]
    for load in loads:
        load.start()
    places = [(f, t) for f in range(5) for t in ts]
    first = (len(places) + 1) // 2
    for i in range(first):
        f, t = places[i]
        body[f, t, LANES:columns, :] = jnp.where(upper, from_west[i], from_east[i])
        if i + first < len(places):
            f, t = places[i + first]
            body[f, t, LANES:columns, :] = half_turn(jnp.where(upper, from_east[i], from_west[i]))
    for load in loads:
        load.wait()
    for f in range(5):
        for t in ts:
            body[f, t, columns : columns + SUB, :] = body[f, t, 0:SUB, :]

    def cells(f, c):
        return [body.at[f, t][pl.ds(c, SUB, stride=nc), :] for t in ts]

    def get(place, c):
        return [grid[place][c + 1, t] for t in ts]

    def put(place, c, tiles):
        for t in ts:
            grid[place][c + 1, t] = tiles[t]

    def sweep(before, column):
        def store(lists):
            for ref, tiles in zip(prev, lists):
                for t in ts:
                    ref[t] = tiles[t]

        def some(start, count):
            lists = [[ref[t] for t in ts] for ref in prev]
            for i in range(count):
                lists = column(start + i, lists)
            store(lists)

        def body(i, carry):
            some(i * UNROLL, UNROLL)
            return carry

        store(before)
        lax.fori_loop(0, nc // UNROLL, body, 0)
        if nc % UNROLL:
            some(nc - nc % UNROLL, nc % UNROLL)

    def down(tiles):
        return [pltpu.roll(x, 1, 0) for x in tiles]

    def wrap(place, left=True, right=True):
        if left:
            put(place, -1, down(get(place, nc - 1)))
        if right:
            put(place, nc, [pltpu.roll(x, SUB - 1, 0) for x in get(place, 0)])

    seam_tile = (rows + HALO - 1) % stride
    seam_block = (rows + HALO - 1) // stride
    spare_tile = (rows + 2 * HALO - 1) % stride
    at_seam = (lane % blocks == seam_block) & tops

    def across_flux(c):
        open_c = each(jnp.minimum, cells(4, c), cells(4, c + 1))
        speed = pairs(halves, cells(2, c), open_c)
        return open_c, [pairs(flux_pair, cells(f, c), cells(f, c + 1), *speed) for f in range(2)]

    open_c, flux_c = across_flux(nc - 1)
    put(15, -1, down(open_c))
    for f in range(2):
        put(4 + f, -1, down(flux_c[f][1]))

    before = [down(low) for low, _ in flux_c]

    def upwind_step(c, old):
        open_c, flux_c = across_flux(c)
        m = cells(4, c)
        open_a = each(jnp.minimum, m, ahead(m))
        v = cells(3, c)
        speed = pairs(halves, v, open_a)
        alt = halves(jnp.where(at_seam, v[spare_tile], v[seam_tile]), open_a[seam_tile])
        results = []
        for f in range(2):
            q = cells(f, c)
            q_a = ahead(q)
            low_a, anti_a = pairs(flux_pair, q, q_a, *speed)
            low_alt, anti_alt = flux_pair(q[seam_tile], q_a[seam_tile], *alt)
            low_b = behind(replaced(low_a, {seam_tile: low_alt}))
            low_c, anti_c = flux_c[f]
            results.append((each(net, q, low_a, low_b, low_c, old[f]), anti_a, anti_c, low_c, anti_alt))
        put(14, c, open_a)
        put(15, c, open_c)
        put(16, c, m)
        for f, (upwind, anti_a, anti_c, low_c, anti_alt) in enumerate(results):
            put(f, c, upwind)
            put(2 + f, c, anti_a)
            put(4 + f, c, anti_c)
            alts[f][c] = anti_alt
        return [x[3] for x in results]

    sweep(before, upwind_step)
    wrap(0)
    wrap(1)

    def across_step(f, c):
        return each(lambda u, n, m: jnp.where(m > 0.0, n - u, 0.0), get(f, c), get(f, c + 1), get(15, c))

    def ratio_step(c, old):
        open_a = get(14, c)
        results = []
        for f in range(2):
            up = get(f, c)
            step_a = each(lambda u, n, m: jnp.where(m > 0.0, n - u, 0.0), up, ahead(up), open_a)
            step_c = across_step(f, c)
            anti_a = get(2 + f, c)
            anti_b = behind(replaced(anti_a, {seam_tile: alts[f][c]}))
            plus, minus = pairs(
                ratios, anti_a, anti_b, get(4 + f, c), get(4 + f, c - 1),
                step_a, behind(step_a), step_c, old[f],
            )
            results.append((plus, minus, step_c))
        for f, (plus, minus, step_c) in enumerate(results):
            put(6 + f, c, plus)
            put(8 + f, c, minus)
        return [x[2] for x in results]

    sweep([across_step(f, -1) for f in range(2)], ratio_step)
    for place in range(6, 10):
        wrap(place)

    def across_limited(f, c):
        return each(limited_flux, get(4 + f, c), get(6 + f, c), get(8 + f, c), get(6 + f, c + 1), get(8 + f, c + 1))

    def advect_step(c, old):
        m = get(16, c)
        results = []
        for f in range(2):
            plus, minus = get(6 + f, c), get(8 + f, c)
            plus_a, minus_a = ahead(plus), ahead(minus)
            lim_a = each(limited_flux, get(2 + f, c), plus, minus, plus_a, minus_a)
            s = seam_tile
            lim_alt = limited_flux(alts[f][c], plus[s], minus[s], plus_a[s], minus_a[s])
            lim_c = across_limited(f, c)
            new = each(net, get(f, c), lim_a, behind(replaced(lim_a, {s: lim_alt})), lim_c, old[f])
            step = each(lambda x, n: jnp.where(n > 1.0, pltpu.roll(x, LANES - blocks, 1) - x, 0.0), new, m)
            results.append((new, step, lim_c))
        for f, (new, step, lim_c) in enumerate(results):
            put(10 + f, c, new)
            put(12 + f, c, step)
        return [x[2] for x in results]

    sweep([across_limited(f, -1) for f in range(2)], advect_step)
    for place in range(10, 14):
        wrap(place)

    def across_face(c):
        sides = [get(place, at) for place in (10, 11, 12, 13) for at in (c, c + 1)]
        return pairs(face, *sides, get(15, c))

    def diffuse_step(c, old):
        values = [get(place, c) for place in (10, 11, 12, 13)]
        sides = [side for x in values for side in (x, ahead(x))]
        flux_a = pairs(face, *sides, get(14, c))
        flux_c = across_face(c)
        new = [
            each(
                lambda q, a, b, x, y: q + DIFFUSIVITY * ((a - b) + (x - y)),
                values[f], flux_a[f], behind(flux_a[f]), flux_c[f], old[f],
            )
            for f in range(2)
        ]
        for f in range(2):
            for t in ts:
                result.at[f, t][pl.ds(c, SUB, stride=nc), :] = new[f][t]
        return flux_c

    sweep(across_face(-1), diffuse_step)

    stores = []
    for f, ref in enumerate((temp_out, salt_out)):

        for t in ts:
            flat.at[f][pl.ds(HALO + t, LANES, stride=stride), :] = result[f, t, 0:LANES, :].T

        def collect(k, carry):
            for t in range(rows // SUB):
                at = HALO + HALO + k * period + t * SUB
                out[f, k, t * SUB : t * SUB + SUB, :] = flat[f, pl.ds(at, SUB), :]
            return carry

        lax.fori_loop(0, levels, collect, 0, unroll=4)
        store = pltpu.make_async_copy(out.at[f], ref, sems.at[f])
        store.start()
        stores.append(store)
    for store in stores:
        store.wait()


def local(nl, nlat, temp, salt, east, north, indicator, total, seam):
    levels, rows, width = temp.shape
    half = 2 * levels
    blocks, stride, period, length = stretch(levels, rows)
    vmem = pl.BlockSpec(memory_space=pltpu.VMEM)
    smem = pl.BlockSpec(memory_space=pltpu.SMEM)
    anywhere = pl.BlockSpec(memory_space=pl.ANY)
    f32 = jnp.float32

    def params(mib):
        return pltpu.CompilerParams(vmem_limit_bytes=mib * 1024 * 1024)

    last = rows // SUB - 1
    low = pl.BlockSpec((levels, SUB, width), lambda i: (0, 0, 0))
    high = pl.BlockSpec((levels, SUB, width), lambda i: (0, last, 0))
    flat_low = pl.BlockSpec((SUB, width), lambda i: (0, 0))
    flat_high = pl.BlockSpec((SUB, width), lambda i: (last, 0))
    block = jax.ShapeDtypeStruct((half + 1, SUB, width), f32)
    whole_block = pl.BlockSpec((half + 1, SUB, width), lambda i: (0, 0, 0))
    fields = (temp, salt, east, north)
    first, second, turn = pl.pallas_call(
        functools.partial(pack_rows, levels, width),
        grid=(1,),
        in_specs=[smem] + [low] * 4 + [high] * 4 + [flat_low, flat_high] * 2,
        out_specs=[whole_block] * 2 + [smem],
        out_shape=[block] * 2 + [jax.ShapeDtypeStruct((1,), jnp.int32)],
        compiler_params=params(56),
    )(seam, *fields, *fields, indicator, indicator, total, total)

    q1 = lax.ppermute(first, "lat", [(j, j ^ 1) for j in range(nlat)])

    def meet(turned):
        def facing(back):
            return [(i * nlat + nlat - 1, (turned - back - i) % nl * nlat + nlat - 1) for i in range(nl)]

        inner = [(i * nlat + j, i * nlat + (j + 1 if j % 2 else j - 1)) for i in range(nl) for j in range(1, nlat - 1)]

        def send(x):
            return lax.ppermute(x, ("lon", "lat"), inner + facing(0)), lax.ppermute(x, ("lon", "lat"), facing(1))

        return send

    q2, q3 = lax.switch(turn[0], [meet(t) for t in range(nl)], second)

    payload = jax.ShapeDtypeStruct(((5 * stride + 1) // 2, SUB, width), f32)
    turned, to_east, to_west = pl.pallas_call(
        functools.partial(turn_fields, levels, rows),
        in_specs=[smem] + [vmem] * 9,
        out_specs=[vmem] * 3,
        out_shape=[jax.ShapeDtypeStruct((5, stride, width, LANES), f32), payload, payload],
        scratch_shapes=[
            pltpu.VMEM((5, length, width), f32),
            pltpu.VMEM((half + 1, SUB, width), f32),
            pltpu.VMEM((SUB, width), f32),
        ],
        compiler_params=params(20),
    )(seam, *fields, indicator, total, q1, q2, q3)
    from_west = lax.ppermute(to_east, "lon", [(i, (i + 1) % nl) for i in range(nl)])
    from_east = lax.ppermute(to_west, "lon", [((i + 1) % nl, i) for i in range(nl)])

    columns = width + 2 * HALO
    nc = columns // SUB
    return pl.pallas_call(
        functools.partial(step, levels, rows),
        in_specs=[anywhere, vmem, vmem],
        out_specs=[anywhere] * 2,
        out_shape=[jax.ShapeDtypeStruct(temp.shape, f32)] * 2,
        scratch_shapes=[
            pltpu.VMEM((5, stride, columns + SUB, LANES), f32),
            pltpu.VMEM((2, stride, columns, LANES), f32),
            pltpu.VMEM((2, length, width), f32),
            pltpu.VMEM((2, levels, rows, width), f32),
            pltpu.SemaphoreType.DMA((5,)),
        ]
        + [pltpu.VMEM((nc + 2, stride, SUB, LANES), f32)] * 17
        + [pltpu.VMEM((nc, SUB, LANES), f32)] * 2
        + [pltpu.VMEM((stride, SUB, LANES), f32)] * 2,
        compiler_params=params(40),
    )(turned, from_east, from_west)


def solution(mesh):
    in_specs = (
        P(None, "lat", "lon"),
        P(None, "lat", "lon"),
        P(None, "lat", "lon"),
        P(None, "lat", "lon"),
        P("lat", "lon"),
        P("lat", "lon"),
        P(),
    )
    out_specs = (P(None, "lat", "lon"), P(None, "lat", "lon"))
    body = functools.partial(local, mesh.shape["lon"], mesh.shape["lat"])
    return jax.shard_map(body, mesh=mesh, in_specs=in_specs, out_specs=out_specs, check_vma=False)
```

```python
import functools

import jax
import jax.numpy as jnp
from jax import lax
from jax.experimental import pallas as pl
from jax.experimental.pallas import tpu as pltpu
from jax.sharding import PartitionSpec as P

RATIO_FLOOR = 0.05
DIFFUSIVITY = 0.1
THERMAL_COEF = 0.2
HALINE_COEF = 0.8

UNROLL = 6
HALO = 4
SUB = 8
LANES = 128


def sublanes():
    return lax.broadcasted_iota(jnp.int32, (SUB, LANES), 0)


def lanes():
    return lax.broadcasted_iota(jnp.int32, (SUB, LANES), 1)


def half_turn(tile):
    return pltpu.roll(tile, 4, 0)


def as_mask(flag):
    return (jnp.zeros((SUB, LANES), jnp.int32) + flag) > 0


def wet_count(indicator, total):
    return jnp.where(indicator == 1, total, 0).astype(jnp.float32)


def pack_rows(levels, width, seam, *refs):
    south, north, (ind_s, ind_n, tot_s, tot_n), (first, second, turn) = refs[:4], refs[4:8], refs[8:12], refs[12:]
    turn[0] = lax.div(seam[0], width)
    lat = lax.axis_index("lat")
    odd = as_mask(lat % 2)
    upper = sublanes() >= HALO
    for i in range(2 * levels):
        f, k = divmod(i, levels)
        low = jnp.where(upper, half_turn(south[f + 2][k]), south[f][k])
        high = jnp.where(upper, north[f][k], half_turn(north[f + 2][k]))
        first[i] = jnp.where(odd, low, high)
        second[i] = jnp.where(odd, high, low)
    low = wet_count(ind_s[...], tot_s[...])
    high = wet_count(ind_n[...], tot_n[...])
    first[2 * levels] = jnp.where(odd, low, high)
    second[2 * levels] = jnp.where(odd, high, low)

    @pl.when(lat == lax.axis_size("lat") - 1)
    def _():
        for i in range(2 * levels):
            f, k = divmod(i, levels)
            for j in range(HALO):
                second[i, j : j + 1, :] = north[f][k, 7 - j : 8 - j, :]
                row = 7 - j if f == 0 else (6, 5, 4, 7)[j]
                second[i, HALO + j : HALO + j + 1, :] = -north[f + 2][k, row : row + 1, :]
        for j in range(HALO):
            second[2 * levels, j : j + 1, :] = wet_count(ind_n[7 - j : 8 - j, :], tot_n[7 - j : 8 - j, :])


def stretch(levels, rows):
    blocks = LANES // levels
    stride = -(-(rows + 2 * HALO) // blocks)
    return blocks, stride, blocks * stride, -(-(HALO + stride * LANES) // SUB) * SUB


def turn_fields(levels, rows, seam, *refs):
    fields, ind, tot, block, q1, q2, q3, turned, to_east, to_west, flat, north_halo, spare = refs[:4], *refs[4:]
    blocks, stride, period, length = stretch(levels, rows)
    half = 2 * levels
    nl = lax.axis_size("lon")
    lat = lax.axis_index("lat")
    odd = as_mask(lat % 2)
    closed = as_mask((lat == 0).astype(jnp.int32))
    lane = lanes()
    upper = sublanes() >= HALO

    def south_halo(i):
        return jnp.where(closed, 0.0, jnp.where(odd, q1[i], q2[i]))

    for i in range(half + 1):
        north_halo[i] = jnp.where(odd, q2[i], q1[i])

    @pl.when(lat == lax.axis_size("lat") - 1)
    def _():
        r = seam[0] & (LANES - 1)
        at_home = lax.rem(lax.div(seam[0], LANES) - 2 * lax.axis_index("lon") + 2 * nl, nl)
        first_own = as_mask((at_home == 0).astype(jnp.int32))
        second_own = as_mask((at_home == 1).astype(jnp.int32))
        for i in range(half + 1):
            at = r - lane - jnp.where(upper, 1 if i < levels else 0, 0)
            index = at & (LANES - 1)

            def pick(tile):
                return jnp.take_along_axis(tile, index, axis=1, mode="promise_in_bounds")

            here = pick(jnp.where(first_own, block[i], q2[i]))
            north_halo[i] = jnp.where(at < 0, pick(jnp.where(second_own, block[i], q3[i])), here)

    tiles = rows // SUB
    for f in range(4):

        def fill(k, carry):
            at = HALO + HALO + k * period
            for t in range(tiles):
                flat[f, pl.ds(at + t * SUB, SUB), :] = fields[f][k, t * SUB : t * SUB + SUB, :]
            i = (f % 2) * levels + k
            n_tile, s_tile = north_halo[i], south_halo(i)
            if f >= 2:
                n_tile, s_tile = half_turn(n_tile), half_turn(s_tile)
            flat[f, pl.ds(at - SUB, SUB), :] = jnp.where(upper, s_tile, 0.0)
            flat[f, pl.ds(at + rows, SUB), :] = jnp.where(upper, 0.0, n_tile)
            return carry

        lax.fori_loop(0, levels, fill, 0, unroll=4)
    for t in range(tiles + 2):
        if t == 0:
            n = jnp.where(upper, south_halo(half), 0.0)
        elif t == tiles + 1:
            n = jnp.where(upper, 0.0, north_halo[half])
        else:
            n = wet_count(ind[t * SUB - SUB : t * SUB, :], tot[t * SUB - SUB : t * SUB, :])

        def left_over(k, carry):
            flat[4, pl.ds(HALO + HALO + k * period + (t - 1) * SUB, SUB), :] = n - k.astype(jnp.float32)
            return carry

        lax.fori_loop(0, levels, left_over, 0, unroll=4)
    end = levels * period
    for f in range(5):
        for t in range(end // SUB * SUB, length, SUB):
            keep = sublanes() + t < end
            flat[f, t : t + SUB, :] = jnp.where(keep, flat[f, t : t + SUB, :], 0.0)

    for t in range(stride):
        for f in range(5):
            turned[f, t] = flat.at[f][pl.ds(HALO + t, LANES, stride=stride), :].T

    places = [(f, t) for f in range(5) for t in range(stride)]
    first = (len(places) + 1) // 2
    for i in range(first):
        f, t = places[i]
        west, east = turned[f, t, 0:SUB, :], turned[f, t, LANES - SUB : LANES, :]
        if i + first < len(places):
            f, t = places[i + first]
            west = jnp.where(upper, half_turn(turned[f, t, 0:SUB, :]), west)
            east = jnp.where(upper, east, half_turn(turned[f, t, LANES - SUB : LANES, :]))
        to_west[i] = west
        to_east[i] = east


def ahead(tiles):
    return tiles[1:] + [pltpu.roll(tiles[0], LANES - 1, 1)]


def behind(tiles):
    return [pltpu.roll(tiles[-1], 1, 1)] + tiles[:-1]


def each(function, *lists):
    return [function(*items) for items in zip(*lists)]


def pairs(function, *lists):
    return tuple(map(list, zip(*each(function, *lists))))


def replaced(tiles, other):
    return [other.get(t, x) for t, x in enumerate(tiles)]


def flux_pair(q, q_next, half_speed, half_size):
    anti = half_size * (q_next - q)
    return half_speed * (q_next + q) - anti, anti


def limited_flux(anti, plus, minus, plus_next, minus_next):
    return anti * jnp.where(anti >= 0.0, jnp.minimum(plus_next, minus), jnp.minimum(plus, minus_next))


def reciprocal(x):
    return pl.reciprocal(x, approx=True)


def halves(speed, mask):
    half = jnp.where(mask > 0.0, 0.5 * speed, 0.0)
    return half, jnp.abs(half)


def net(q, a, b, c, d):
    return q - ((a - b) + (c - d))


def ratios(a, b, c, l, sa, sb, sc, sl):
    inflow = (jnp.maximum(b, 0.0) - jnp.minimum(a, 0.0)) + (jnp.maximum(l, 0.0) - jnp.minimum(c, 0.0))
    outflow = (jnp.maximum(a, 0.0) - jnp.minimum(b, 0.0)) + (jnp.maximum(c, 0.0) - jnp.minimum(l, 0.0))
    rise = jnp.maximum(jnp.maximum(jnp.maximum(sa, sc), 0.0), -jnp.minimum(sb, sl))
    drop = jnp.maximum(jnp.maximum(jnp.maximum(sb, sl), 0.0), -jnp.minimum(sa, sc))
    plus = jnp.minimum(1.0, rise * reciprocal(jnp.maximum(inflow, RATIO_FLOOR)))
    minus = jnp.minimum(1.0, drop * reciprocal(jnp.maximum(outflow, RATIO_FLOOR)))
    return plus, minus


def face(t0, t1, s0, s1, zt0, zt1, zs0, zs1, m):
    dt, ds, zt, zs = t1 - t0, s1 - s0, zt1 + zt0, zs1 + zs0
    bottom = jnp.maximum(HALINE_COEF * zs - THERMAL_COEF * zt, 1.0)
    half_slope = (HALINE_COEF * ds - THERMAL_COEF * dt) * reciprocal(bottom)
    half_slope = jnp.maximum(jnp.minimum(half_slope, 1.0), -1.0)
    return jnp.where(m > 0.0, dt - half_slope * zt, 0.0), jnp.where(m > 0.0, ds - half_slope * zs, 0.0)


def step(levels, rows, *refs):
    (
        turned, from_east, from_west, temp_out, salt_out,
        body, result, flat, out, sems, *grid
    ) = refs
    grid, alts, prev = grid[:17], grid[17:19], grid[19:]
    blocks, stride, period, length = stretch(levels, rows)
    columns = LANES + 2 * HALO
    nc = columns // SUB
    ts = range(stride)
    lat = lax.axis_index("lat")
    tops = as_mask((lat == lax.axis_size("lat") - 1).astype(jnp.int32))
    lane = lanes()
    upper = sublanes() >= HALO
    loads = [
        pltpu.make_async_copy(turned.at[f], body.at[f, :, 0:LANES, :], sems.at[f]) for f in range(5)
    ]
    for load in loads:
        load.start()
    places = [(f, t) for f in range(5) for t in ts]
    first = (len(places) + 1) // 2
    for i in range(first):
        f, t = places[i]
        body[f, t, LANES:columns, :] = jnp.where(upper, from_west[i], from_east[i])
        if i + first < len(places):
            f, t = places[i + first]
            body[f, t, LANES:columns, :] = half_turn(jnp.where(upper, from_east[i], from_west[i]))
    for load in loads:
        load.wait()
    for f in range(5):
        for t in ts:
            body[f, t, columns : columns + SUB, :] = body[f, t, 0:SUB, :]

    def cells(f, c):
        return [body.at[f, t][pl.ds(c, SUB, stride=nc), :] for t in ts]

    def get(place, c):
        return [grid[place][c + 1, t] for t in ts]

    def put(place, c, tiles):
        for t in ts:
            grid[place][c + 1, t] = tiles[t]

    def sweep(before, column):
        def store(lists):
            for ref, tiles in zip(prev, lists):
                for t in ts:
                    ref[t] = tiles[t]

        def some(start, count):
            lists = [[ref[t] for t in ts] for ref in prev]
            for i in range(count):
                lists = column(start + i, lists)
            store(lists)

        def body(i, carry):
            some(i * UNROLL, UNROLL)
            return carry

        store(before)
        lax.fori_loop(0, nc // UNROLL, body, 0)
        if nc % UNROLL:
            some(nc - nc % UNROLL, nc % UNROLL)

    def down(tiles):
        return [pltpu.roll(x, 1, 0) for x in tiles]

    def wrap(place, left=True, right=True):
        if left:
            put(place, -1, down(get(place, nc - 1)))
        if right:
            put(place, nc, [pltpu.roll(x, SUB - 1, 0) for x in get(place, 0)])

    seam_tile = (rows + HALO - 1) % stride
    seam_block = (rows + HALO - 1) // stride
    spare_tile = (rows + 2 * HALO - 1) % stride
    at_seam = (lane % blocks == seam_block) & tops

    def across_flux(c):
        open_c = each(jnp.minimum, cells(4, c), cells(4, c + 1))
        speed = pairs(halves, cells(2, c), open_c)
        return open_c, [pairs(flux_pair, cells(f, c), cells(f, c + 1), *speed) for f in range(2)]

    open_c, flux_c = across_flux(nc - 1)
    put(15, -1, down(open_c))
    for f in range(2):
        put(4 + f, -1, down(flux_c[f][1]))

    before = [down(low) for low, _ in flux_c]

    def upwind_step(c, old):
        open_c, flux_c = across_flux(c)
        m = cells(4, c)
        open_a = each(jnp.minimum, m, ahead(m))
        v = cells(3, c)
        speed = pairs(halves, v, open_a)
        alt = halves(jnp.where(at_seam, v[spare_tile], v[seam_tile]), open_a[seam_tile])
        results = []
        for f in range(2):
            q = cells(f, c)
            q_a = ahead(q)
            low_a, anti_a = pairs(flux_pair, q, q_a, *speed)
            low_alt, anti_alt = flux_pair(q[seam_tile], q_a[seam_tile], *alt)
            low_b = behind(replaced(low_a, {seam_tile: low_alt}))
            low_c, anti_c = flux_c[f]
            results.append((each(net, q, low_a, low_b, low_c, old[f]), anti_a, anti_c, low_c, anti_alt))
        put(14, c, open_a)
        put(15, c, open_c)
        put(16, c, m)
        for f, (upwind, anti_a, anti_c, low_c, anti_alt) in enumerate(results):
            put(f, c, upwind)
            put(2 + f, c, anti_a)
            put(4 + f, c, anti_c)
            alts[f][c] = anti_alt
        return [x[3] for x in results]

    sweep(before, upwind_step)
    wrap(0)
    wrap(1)

    def across_step(f, c):
        return each(lambda u, n, m: jnp.where(m > 0.0, n - u, 0.0), get(f, c), get(f, c + 1), get(15, c))

    def ratio_step(c, old):
        open_a = get(14, c)
        results = []
        for f in range(2):
            up = get(f, c)
            step_a = each(lambda u, n, m: jnp.where(m > 0.0, n - u, 0.0), up, ahead(up), open_a)
            step_c = across_step(f, c)
            anti_a = get(2 + f, c)
            anti_b = behind(replaced(anti_a, {seam_tile: alts[f][c]}))
            plus, minus = pairs(
                ratios, anti_a, anti_b, get(4 + f, c), get(4 + f, c - 1),
                step_a, behind(step_a), step_c, old[f],
            )
            results.append((plus, minus, step_c))
        for f, (plus, minus, step_c) in enumerate(results):
            put(6 + f, c, plus)
            put(8 + f, c, minus)
        return [x[2] for x in results]

    sweep([across_step(f, -1) for f in range(2)], ratio_step)
    for place in range(6, 10):
        wrap(place)

    def across_limited(f, c):
        return each(limited_flux, get(4 + f, c), get(6 + f, c), get(8 + f, c), get(6 + f, c + 1), get(8 + f, c + 1))

    def advect_step(c, old):
        m = get(16, c)
        results = []
        for f in range(2):
            plus, minus = get(6 + f, c), get(8 + f, c)
            plus_a, minus_a = ahead(plus), ahead(minus)
            lim_a = each(limited_flux, get(2 + f, c), plus, minus, plus_a, minus_a)
            s = seam_tile
            lim_alt = limited_flux(alts[f][c], plus[s], minus[s], plus_a[s], minus_a[s])
            lim_c = across_limited(f, c)
            new = each(net, get(f, c), lim_a, behind(replaced(lim_a, {s: lim_alt})), lim_c, old[f])
            step = each(lambda x, n: jnp.where(n > 1.0, pltpu.roll(x, LANES - blocks, 1) - x, 0.0), new, m)
            results.append((new, step, lim_c))
        for f, (new, step, lim_c) in enumerate(results):
            put(10 + f, c, new)
            put(12 + f, c, step)
        return [x[2] for x in results]

    sweep([across_limited(f, -1) for f in range(2)], advect_step)
    for place in range(10, 14):
        wrap(place)

    def across_face(c):
        sides = [get(place, at) for place in (10, 11, 12, 13) for at in (c, c + 1)]
        return pairs(face, *sides, get(15, c))

    def diffuse_step(c, old):
        values = [get(place, c) for place in (10, 11, 12, 13)]
        sides = [side for x in values for side in (x, ahead(x))]
        flux_a = pairs(face, *sides, get(14, c))
        flux_c = across_face(c)
        new = [
            each(
                lambda q, a, b, x, y: q + DIFFUSIVITY * ((a - b) + (x - y)),
                values[f], flux_a[f], behind(flux_a[f]), flux_c[f], old[f],
            )
            for f in range(2)
        ]
        for f in range(2):
            for t in ts:
                result.at[f, t][pl.ds(c, SUB, stride=nc), :] = new[f][t]
        return flux_c

    sweep(across_face(-1), diffuse_step)

    stores = []
    for f, ref in enumerate((temp_out, salt_out)):

        for t in ts:
            flat.at[f][pl.ds(HALO + t, LANES, stride=stride), :] = result[f, t, 0:LANES, :].T

        def collect(k, carry):
            for t in range(rows // SUB):
                at = HALO + HALO + k * period + t * SUB
                out[f, k, t * SUB : t * SUB + SUB, :] = flat[f, pl.ds(at, SUB), :]
            return carry

        lax.fori_loop(0, levels, collect, 0, unroll=4)
        store = pltpu.make_async_copy(out.at[f], ref, sems.at[f])
        store.start()
        stores.append(store)
    for store in stores:
        store.wait()


def local(nl, nlat, temp, salt, east, north, indicator, total, seam):
    levels, rows, width = temp.shape
    half = 2 * levels
    blocks, stride, period, length = stretch(levels, rows)
    vmem = pl.BlockSpec(memory_space=pltpu.VMEM)
    smem = pl.BlockSpec(memory_space=pltpu.SMEM)
    anywhere = pl.BlockSpec(memory_space=pl.ANY)
    f32 = jnp.float32

    def params(mib):
        return pltpu.CompilerParams(vmem_limit_bytes=mib * 1024 * 1024)

    last = rows // SUB - 1
    low = pl.BlockSpec((levels, SUB, width), lambda i: (0, 0, 0))
    high = pl.BlockSpec((levels, SUB, width), lambda i: (0, last, 0))
    flat_low = pl.BlockSpec((SUB, width), lambda i: (0, 0))
    flat_high = pl.BlockSpec((SUB, width), lambda i: (last, 0))
    block = jax.ShapeDtypeStruct((half + 1, SUB, width), f32)
    whole_block = pl.BlockSpec((half + 1, SUB, width), lambda i: (0, 0, 0))
    fields = (temp, salt, east, north)
    first, second, turn = pl.pallas_call(
        functools.partial(pack_rows, levels, width),
        grid=(1,),
        in_specs=[smem] + [low] * 4 + [high] * 4 + [flat_low, flat_high] * 2,
        out_specs=[whole_block] * 2 + [smem],
        out_shape=[block] * 2 + [jax.ShapeDtypeStruct((1,), jnp.int32)],
        compiler_params=params(56),
    )(seam, *fields, *fields, indicator, indicator, total, total)

    q1 = lax.ppermute(first, "lat", [(j, j ^ 1) for j in range(nlat)])

    def meet(turned):
        def facing(back):
            pairs = []
            for i in range(nl):
                to = (turned - back - i) % nl
                to = (i + nl // 2) % nl if to == i else to
                pairs.append((i * nlat + nlat - 1, to * nlat + nlat - 1))
            return pairs

        def idle(rows):
            return [(i * nlat + j, (i ^ 1) * nlat + j) for i in range(nl) for j in rows]

        inner = [(i * nlat + j, i * nlat + (j + 1 if j % 2 else j - 1)) for i in range(nl) for j in range(1, nlat - 1)]

        def send(x):
            return (
                lax.ppermute(x, ("lon", "lat"), idle([0]) + inner + facing(0)),
                lax.ppermute(x, ("lon", "lat"), idle(range(nlat - 1)) + facing(1)),
            )

        return send

    q2, q3 = lax.switch(turn[0], [meet(t) for t in range(nl)], second)

    payload = jax.ShapeDtypeStruct(((5 * stride + 1) // 2, SUB, width), f32)
    turned, to_east, to_west = pl.pallas_call(
        functools.partial(turn_fields, levels, rows),
        in_specs=[smem] + [vmem] * 10,
        out_specs=[vmem] * 3,
        out_shape=[jax.ShapeDtypeStruct((5, stride, width, LANES), f32), payload, payload],
        scratch_shapes=[
            pltpu.VMEM((5, length, width), f32),
            pltpu.VMEM((half + 1, SUB, width), f32),
            pltpu.VMEM((SUB, width), f32),
        ],
        compiler_params=params(20),
    )(seam, *fields, indicator, total, second, q1, q2, q3)
    from_west = lax.ppermute(to_east, "lon", [(i, (i + 1) % nl) for i in range(nl)])
    from_east = lax.ppermute(to_west, "lon", [((i + 1) % nl, i) for i in range(nl)])

    columns = width + 2 * HALO
    nc = columns // SUB
    return pl.pallas_call(
        functools.partial(step, levels, rows),
        in_specs=[anywhere, vmem, vmem],
        out_specs=[anywhere] * 2,
        out_shape=[jax.ShapeDtypeStruct(temp.shape, f32)] * 2,
        scratch_shapes=[
            pltpu.VMEM((5, stride, columns + SUB, LANES), f32),
            pltpu.VMEM((2, stride, columns, LANES), f32),
            pltpu.VMEM((2, length, width), f32),
            pltpu.VMEM((2, levels, rows, width), f32),
            pltpu.SemaphoreType.DMA((5,)),
        ]
        + [pltpu.VMEM((nc + 2, stride, SUB, LANES), f32)] * 17
        + [pltpu.VMEM((nc, SUB, LANES), f32)] * 2
        + [pltpu.VMEM((stride, SUB, LANES), f32)] * 2,
        compiler_params=params(40),
    )(turned, from_east, from_west)


def solution(mesh):
    in_specs = (
        P(None, "lat", "lon"),
        P(None, "lat", "lon"),
        P(None, "lat", "lon"),
        P(None, "lat", "lon"),
        P("lat", "lon"),
        P("lat", "lon"),
        P(),
    )
    out_specs = (P(None, "lat", "lon"), P(None, "lat", "lon"))
    body = functools.partial(local, mesh.shape["lon"], mesh.shape["lat"])
    return jax.shard_map(body, mesh=mesh, in_specs=in_specs, out_specs=out_specs, check_vma=False)
```

```python
import functools

import jax
import jax.numpy as jnp
from jax import lax
from jax.experimental import pallas as pl
from jax.experimental.pallas import tpu as pltpu
from jax.sharding import PartitionSpec as P

RATIO_FLOOR = 0.05
DIFFUSIVITY = 0.1
THERMAL_COEF = 0.2
HALINE_COEF = 0.8

BATCH = 3
UNROLL = 6
HALO = 4
SUB = 8
LANES = 128


def sublanes():
    return lax.broadcasted_iota(jnp.int32, (SUB, LANES), 0)


def lanes():
    return lax.broadcasted_iota(jnp.int32, (SUB, LANES), 1)


def half_turn(tile):
    return pltpu.roll(tile, 4, 0)


def as_mask(flag):
    return (jnp.zeros((SUB, LANES), jnp.int32) + flag) > 0


def wet_count(indicator, total):
    return jnp.where(indicator == 1, total, 0).astype(jnp.float32)


def pack_rows(levels, width, seam, *refs):
    south, north, (ind_s, ind_n, tot_s, tot_n), (first, second, turn) = refs[:4], refs[4:8], refs[8:12], refs[12:]
    turn[0] = lax.div(seam[0], width)
    lat = lax.axis_index("lat")
    odd = as_mask(lat % 2)
    upper = sublanes() >= HALO
    for i in range(2 * levels):
        f, k = divmod(i, levels)
        low = jnp.where(upper, half_turn(south[f + 2][k]), south[f][k])
        high = jnp.where(upper, north[f][k], half_turn(north[f + 2][k]))
        first[i] = jnp.where(odd, low, high)
        second[i] = jnp.where(odd, high, low)
    low = wet_count(ind_s[...], tot_s[...])
    high = wet_count(ind_n[...], tot_n[...])
    first[2 * levels] = jnp.where(odd, low, high)
    second[2 * levels] = jnp.where(odd, high, low)

    @pl.when(lat == lax.axis_size("lat") - 1)
    def _():
        for i in range(2 * levels):
            f, k = divmod(i, levels)
            for j in range(HALO):
                second[i, j : j + 1, :] = north[f][k, 7 - j : 8 - j, :]
                row = 7 - j if f == 0 else (6, 5, 4, 7)[j]
                second[i, HALO + j : HALO + j + 1, :] = -north[f + 2][k, row : row + 1, :]
        for j in range(HALO):
            second[2 * levels, j : j + 1, :] = wet_count(ind_n[7 - j : 8 - j, :], tot_n[7 - j : 8 - j, :])


def stretch(levels, rows):
    blocks = LANES // levels
    stride = -(-(rows + 2 * HALO) // blocks)
    return blocks, stride, blocks * stride, -(-(HALO + stride * LANES) // SUB) * SUB


def turn_fields(levels, rows, seam, *refs):
    fields, ind, tot, block, q1, q2, q3, turned, to_east, to_west, flat, north_halo, spare = refs[:4], *refs[4:]
    blocks, stride, period, length = stretch(levels, rows)
    half = 2 * levels
    nl = lax.axis_size("lon")
    lat = lax.axis_index("lat")
    odd = as_mask(lat % 2)
    closed = as_mask((lat == 0).astype(jnp.int32))
    lane = lanes()
    upper = sublanes() >= HALO

    def south_halo(i):
        return jnp.where(closed, 0.0, jnp.where(odd, q1[i], q2[i]))

    for i in range(half + 1):
        north_halo[i] = jnp.where(odd, q2[i], q1[i])

    @pl.when(lat == lax.axis_size("lat") - 1)
    def _():
        r = seam[0] & (LANES - 1)
        at_home = lax.rem(lax.div(seam[0], LANES) - 2 * lax.axis_index("lon") + 2 * nl, nl)
        first_own = as_mask((at_home == 0).astype(jnp.int32))
        second_own = as_mask((at_home == 1).astype(jnp.int32))
        for i in range(half + 1):
            at = r - lane - jnp.where(upper, 1 if i < levels else 0, 0)
            index = at & (LANES - 1)

            def pick(tile):
                return jnp.take_along_axis(tile, index, axis=1, mode="promise_in_bounds")

            here = pick(jnp.where(first_own, block[i], q2[i]))
            north_halo[i] = jnp.where(at < 0, pick(jnp.where(second_own, block[i], q3[i])), here)

    tiles = rows // SUB
    for f in range(4):

        def fill(k, carry):
            at = HALO + HALO + k * period
            for t in range(tiles):
                flat[f, pl.ds(at + t * SUB, SUB), :] = fields[f][k, t * SUB : t * SUB + SUB, :]
            i = (f % 2) * levels + k
            n_tile, s_tile = north_halo[i], south_halo(i)
            if f >= 2:
                n_tile, s_tile = half_turn(n_tile), half_turn(s_tile)
            flat[f, pl.ds(at - SUB, SUB), :] = jnp.where(upper, s_tile, 0.0)
            flat[f, pl.ds(at + rows, SUB), :] = jnp.where(upper, 0.0, n_tile)
            return carry

        lax.fori_loop(0, levels, fill, 0, unroll=12)
    for t in range(tiles + 2):
        if t == 0:
            n = jnp.where(upper, south_halo(half), 0.0)
        elif t == tiles + 1:
            n = jnp.where(upper, 0.0, north_halo[half])
        else:
            n = wet_count(ind[t * SUB - SUB : t * SUB, :], tot[t * SUB - SUB : t * SUB, :])

        def left_over(k, carry):
            flat[4, pl.ds(HALO + HALO + k * period + (t - 1) * SUB, SUB), :] = n - k.astype(jnp.float32)
            return carry

        lax.fori_loop(0, levels, left_over, 0, unroll=12)
    end = levels * period
    for f in range(5):
        for t in range(end // SUB * SUB, length, SUB):
            keep = sublanes() + t < end
            flat[f, t : t + SUB, :] = jnp.where(keep, flat[f, t : t + SUB, :], 0.0)

    for t in range(stride):
        for f in range(5):
            turned[f, t] = flat.at[f][pl.ds(HALO + t, LANES, stride=stride), :].T

    places = [(f, t) for f in range(5) for t in range(stride)]
    first = (len(places) + 1) // 2
    for i in range(first):
        f, t = places[i]
        west, east = turned[f, t, 0:SUB, :], turned[f, t, LANES - SUB : LANES, :]
        if i + first < len(places):
            f, t = places[i + first]
            west = jnp.where(upper, half_turn(turned[f, t, 0:SUB, :]), west)
            east = jnp.where(upper, east, half_turn(turned[f, t, LANES - SUB : LANES, :]))
        to_west[i] = west
        to_east[i] = east


def ahead(tiles):
    return tiles[1:] + [pltpu.roll(tiles[0], LANES - 1, 1)]


def behind(tiles):
    return [pltpu.roll(tiles[-1], 1, 1)] + tiles[:-1]


def each(function, *lists):
    return [function(*items) for items in zip(*lists)]


def pairs(function, *lists):
    return tuple(map(list, zip(*each(function, *lists))))


def replaced(tiles, other):
    return [other.get(t, x) for t, x in enumerate(tiles)]


def flux_pair(q, q_next, half_speed, half_size):
    anti = half_size * (q_next - q)
    return half_speed * (q_next + q) - anti, anti


def limited_flux(anti, plus, minus, plus_next, minus_next):
    return anti * jnp.where(anti >= 0.0, jnp.minimum(plus_next, minus), jnp.minimum(plus, minus_next))


def reciprocal(x):
    return pl.reciprocal(x, approx=True)


def halves(speed, mask):
    half = jnp.where(mask > 0.0, 0.5 * speed, 0.0)
    return half, jnp.abs(half)


def net(q, a, b, c, d):
    return q - ((a - b) + (c - d))


def ratios(a, b, c, l, sa, sb, sc, sl):
    inflow = (jnp.maximum(b, 0.0) - jnp.minimum(a, 0.0)) + (jnp.maximum(l, 0.0) - jnp.minimum(c, 0.0))
    outflow = (jnp.maximum(a, 0.0) - jnp.minimum(b, 0.0)) + (jnp.maximum(c, 0.0) - jnp.minimum(l, 0.0))
    rise = jnp.maximum(jnp.maximum(jnp.maximum(sa, sc), 0.0), -jnp.minimum(sb, sl))
    drop = jnp.maximum(jnp.maximum(jnp.maximum(sb, sl), 0.0), -jnp.minimum(sa, sc))
    plus = jnp.minimum(1.0, rise * reciprocal(jnp.maximum(inflow, RATIO_FLOOR)))
    minus = jnp.minimum(1.0, drop * reciprocal(jnp.maximum(outflow, RATIO_FLOOR)))
    return plus, minus


def face(t0, t1, s0, s1, zt0, zt1, zs0, zs1, m):
    dt, ds, zt, zs = t1 - t0, s1 - s0, zt1 + zt0, zs1 + zs0
    bottom = jnp.maximum(HALINE_COEF * zs - THERMAL_COEF * zt, 1.0)
    half_slope = (HALINE_COEF * ds - THERMAL_COEF * dt) * reciprocal(bottom)
    half_slope = jnp.maximum(jnp.minimum(half_slope, 1.0), -1.0)
    return jnp.where(m > 0.0, dt - half_slope * zt, 0.0), jnp.where(m > 0.0, ds - half_slope * zs, 0.0)


def step(levels, rows, *refs):
    (
        turned, from_east, from_west, temp_out, salt_out,
        body, result, flat, out, sems, *grid
    ) = refs
    grid, alts, prev = grid[:17], grid[17:19], grid[19:]
    blocks, stride, period, length = stretch(levels, rows)
    columns = LANES + 2 * HALO
    nc = columns // SUB
    ts = range(stride)
    lat = lax.axis_index("lat")
    tops = as_mask((lat == lax.axis_size("lat") - 1).astype(jnp.int32))
    lane = lanes()
    upper = sublanes() >= HALO
    loads = [
        pltpu.make_async_copy(turned.at[f], body.at[f, :, 0:LANES, :], sems.at[f]) for f in range(5)
    ]
    for load in loads:
        load.start()
    places = [(f, t) for f in range(5) for t in ts]
    first = (len(places) + 1) // 2
    for i in range(first):
        f, t = places[i]
        body[f, t, LANES:columns, :] = jnp.where(upper, from_west[i], from_east[i])
        if i + first < len(places):
            f, t = places[i + first]
            body[f, t, LANES:columns, :] = half_turn(jnp.where(upper, from_east[i], from_west[i]))
    for load in loads:
        load.wait()
    for f in range(5):
        for t in ts:
            body[f, t, columns : columns + SUB, :] = body[f, t, 0:SUB, :]

    held = {}

    def load(key, c, tile):
        if key + c[1:] not in held:
            held[key + c[1:]] = [tile(sum(c), t) for t in ts]
        return held[key + c[1:]]

    def after(c, n=1):
        return c[0], c[1] + n

    def cells(f, c):
        return load((f, "in"), c, lambda at, t: body.at[f, t][pl.ds(at, SUB, stride=nc), :])

    def get(place, c):
        return load((place,), c, lambda at, t: grid[place][at + 1, t])

    def put(place, c, tiles):
        for t in ts:
            grid[place][sum(c) + 1, t] = tiles[t]

    def sweep(before, column):
        def store(lists):
            for ref, tiles in zip(prev, lists):
                for t in ts:
                    ref[t] = tiles[t]

        def some(start, count):
            held.clear()
            lists = [[ref[t] for t in ts] for ref in prev]
            for i in range(count):
                lists = column((start, i), lists)
            store(lists)
            held.clear()

        def body(i, carry):
            some(i * UNROLL, UNROLL)
            return carry

        store(before)
        lax.fori_loop(0, nc // UNROLL, body, 0)
        if nc % UNROLL:
            some(nc - nc % UNROLL, nc % UNROLL)

    def down(tiles):
        return [pltpu.roll(x, 1, 0) for x in tiles]

    def wrap(*places):
        held.clear()
        for place in places:
            put(place, (0, -1), down(get(place, (0, nc - 1))))
            put(place, (0, nc), [pltpu.roll(x, SUB - 1, 0) for x in get(place, (0, 0))])
        held.clear()

    seam_tile = (rows + HALO - 1) % stride
    seam_block = (rows + HALO - 1) // stride
    spare_tile = (rows + 2 * HALO - 1) % stride
    at_seam = (lane % blocks == seam_block) & tops

    def across_flux(c):
        open_c = each(jnp.minimum, cells(4, c), cells(4, after(c)))
        speed = pairs(halves, cells(2, c), open_c)
        return open_c, [pairs(flux_pair, cells(f, c), cells(f, after(c)), *speed) for f in range(2)]

    open_c, flux_c = across_flux((0, nc - 1))
    put(15, (0, -1), down(open_c))
    for f in range(2):
        put(4 + f, (0, -1), down(flux_c[f][1]))

    before = [down(low) for low, _ in flux_c]

    def upwind_step(c, old):
        open_c, flux_c = across_flux(c)
        m = cells(4, c)
        open_a = each(jnp.minimum, m, ahead(m))
        v = cells(3, c)
        speed = pairs(halves, v, open_a)
        alt = halves(jnp.where(at_seam, v[spare_tile], v[seam_tile]), open_a[seam_tile])
        results = []
        for f in range(2):
            q = cells(f, c)
            q_a = ahead(q)
            low_a, anti_a = pairs(flux_pair, q, q_a, *speed)
            low_alt, anti_alt = flux_pair(q[seam_tile], q_a[seam_tile], *alt)
            low_b = behind(replaced(low_a, {seam_tile: low_alt}))
            low_c, anti_c = flux_c[f]
            results.append((each(net, q, low_a, low_b, low_c, old[f]), anti_a, anti_c, low_c, anti_alt))
        put(14, c, open_a)
        put(15, c, open_c)
        put(16, c, m)
        for f, (upwind, anti_a, anti_c, low_c, anti_alt) in enumerate(results):
            put(f, c, upwind)
            put(2 + f, c, anti_a)
            put(4 + f, c, anti_c)
            alts[f][sum(c)] = anti_alt
        return [x[3] for x in results]

    sweep(before, upwind_step)
    wrap(0, 1)

    def across_step(f, c):
        return each(lambda u, n, m: jnp.where(m > 0.0, n - u, 0.0), get(f, c), get(f, after(c)), get(15, c))

    def ratio_step(c, old):
        open_a = get(14, c)
        results = []
        for f in range(2):
            up = get(f, c)
            step_a = each(lambda u, n, m: jnp.where(m > 0.0, n - u, 0.0), up, ahead(up), open_a)
            step_c = across_step(f, c)
            anti_a = get(2 + f, c)
            anti_b = behind(replaced(anti_a, {seam_tile: alts[f][sum(c)]}))
            plus, minus = pairs(
                ratios, anti_a, anti_b, get(4 + f, c), get(4 + f, after(c, -1)),
                step_a, behind(step_a), step_c, old[f],
            )
            results.append((plus, minus, step_c))
        for f, (plus, minus, step_c) in enumerate(results):
            put(6 + f, c, plus)
            put(8 + f, c, minus)
        return [x[2] for x in results]

    sweep([across_step(f, (0, -1)) for f in range(2)], ratio_step)
    wrap(6, 7, 8, 9)

    def across_limited(f, c):
        return each(limited_flux, get(4 + f, c), get(6 + f, c), get(8 + f, c), get(6 + f, after(c)), get(8 + f, after(c)))

    def advect_step(c, old):
        m = get(16, c)
        results = []
        for f in range(2):
            plus, minus = get(6 + f, c), get(8 + f, c)
            plus_a, minus_a = ahead(plus), ahead(minus)
            lim_a = each(limited_flux, get(2 + f, c), plus, minus, plus_a, minus_a)
            s = seam_tile
            lim_alt = limited_flux(alts[f][sum(c)], plus[s], minus[s], plus_a[s], minus_a[s])
            lim_c = across_limited(f, c)
            new = each(net, get(f, c), lim_a, behind(replaced(lim_a, {s: lim_alt})), lim_c, old[f])
            step = each(lambda x, n: jnp.where(n > 1.0, pltpu.roll(x, LANES - blocks, 1) - x, 0.0), new, m)
            results.append((new, step, lim_c))
        for f, (new, step, lim_c) in enumerate(results):
            put(10 + f, c, new)
            put(12 + f, c, step)
        return [x[2] for x in results]

    sweep([across_limited(f, (0, -1)) for f in range(2)], advect_step)
    wrap(10, 11, 12, 13)

    def across_face(c):
        sides = [get(place, at) for place in (10, 11, 12, 13) for at in (c, after(c))]
        return pairs(face, *sides, get(15, c))

    def diffuse_step(c, old):
        values = [get(place, c) for place in (10, 11, 12, 13)]
        sides = [side for x in values for side in (x, ahead(x))]
        flux_a = pairs(face, *sides, get(14, c))
        flux_c = across_face(c)
        new = [
            each(
                lambda q, a, b, x, y: q + DIFFUSIVITY * ((a - b) + (x - y)),
                values[f], flux_a[f], behind(flux_a[f]), flux_c[f], old[f],
            )
            for f in range(2)
        ]
        for f in range(2):
            for t in ts:
                result.at[f, t][pl.ds(sum(c), SUB, stride=nc), :] = new[f][t]
        return flux_c

    sweep(across_face((0, -1)), diffuse_step)

    stores = []
    for f, ref in enumerate((temp_out, salt_out)):
        for t in ts:
            flat.at[f][pl.ds(HALO + t, LANES, stride=stride), :] = result[f, t, 0:LANES, :].T
        for g in range(0, levels, BATCH):
            for k in range(g, g + BATCH):
                for t in range(rows // SUB):
                    at = HALO + HALO + k * period + t * SUB
                    out[f, k, t * SUB : t * SUB + SUB, :] = flat[f, at : at + SUB, :]
            levels_of = pl.ds(g, BATCH)
            store = pltpu.make_async_copy(out.at[f, levels_of], ref.at[levels_of], sems.at[len(stores)])
            store.start()
            stores.append(store)
    for store in stores:
        store.wait()


def local(nl, nlat, temp, salt, east, north, indicator, total, seam):
    levels, rows, width = temp.shape
    half = 2 * levels
    blocks, stride, period, length = stretch(levels, rows)
    vmem = pl.BlockSpec(memory_space=pltpu.VMEM)
    smem = pl.BlockSpec(memory_space=pltpu.SMEM)
    anywhere = pl.BlockSpec(memory_space=pl.ANY)
    f32 = jnp.float32

    def params(mib):
        return pltpu.CompilerParams(vmem_limit_bytes=mib * 1024 * 1024)

    last = rows // SUB - 1
    low = pl.BlockSpec((levels, SUB, width), lambda i: (0, 0, 0))
    high = pl.BlockSpec((levels, SUB, width), lambda i: (0, last, 0))
    flat_low = pl.BlockSpec((SUB, width), lambda i: (0, 0))
    flat_high = pl.BlockSpec((SUB, width), lambda i: (last, 0))
    block = jax.ShapeDtypeStruct((half + 1, SUB, width), f32)
    whole_block = pl.BlockSpec((half + 1, SUB, width), lambda i: (0, 0, 0))
    fields = (temp, salt, east, north)
    first, second, turn = pl.pallas_call(
        functools.partial(pack_rows, levels, width),
        grid=(1,),
        in_specs=[smem] + [low] * 4 + [high] * 4 + [flat_low, flat_high] * 2,
        out_specs=[whole_block] * 2 + [smem],
        out_shape=[block] * 2 + [jax.ShapeDtypeStruct((1,), jnp.int32)],
        compiler_params=params(56),
    )(seam, *fields, *fields, indicator, indicator, total, total)

    q1 = lax.ppermute(first, "lat", [(j, j ^ 1) for j in range(nlat)])

    def meet(turned):
        def facing(back):
            pairs = []
            for i in range(nl):
                to = (turned - back - i) % nl
                to = (i + nl // 2) % nl if to == i else to
                pairs.append((i * nlat + nlat - 1, to * nlat + nlat - 1))
            return pairs

        def idle(rows):
            return [(i * nlat + j, (i ^ 1) * nlat + j) for i in range(nl) for j in rows]

        inner = [(i * nlat + j, i * nlat + (j + 1 if j % 2 else j - 1)) for i in range(nl) for j in range(1, nlat - 1)]

        def send(x):
            return (
                lax.ppermute(x, ("lon", "lat"), idle([0]) + inner + facing(0)),
                lax.ppermute(x, ("lon", "lat"), idle(range(nlat - 1)) + facing(1)),
            )

        return send

    q2, q3 = lax.switch(turn[0], [meet(t) for t in range(nl)], second)

    payload = jax.ShapeDtypeStruct(((5 * stride + 1) // 2, SUB, width), f32)
    turned, to_east, to_west = pl.pallas_call(
        functools.partial(turn_fields, levels, rows),
        in_specs=[smem] + [vmem] * 10,
        out_specs=[vmem] * 3,
        out_shape=[jax.ShapeDtypeStruct((5, stride, width, LANES), f32), payload, payload],
        scratch_shapes=[
            pltpu.VMEM((5, length, width), f32),
            pltpu.VMEM((half + 1, SUB, width), f32),
            pltpu.VMEM((SUB, width), f32),
        ],
        compiler_params=params(20),
    )(seam, *fields, indicator, total, second, q1, q2, q3)
    from_west = lax.ppermute(to_east, "lon", [(i, (i + 1) % nl) for i in range(nl)])
    from_east = lax.ppermute(to_west, "lon", [((i + 1) % nl, i) for i in range(nl)])

    columns = width + 2 * HALO
    nc = columns // SUB
    return pl.pallas_call(
        functools.partial(step, levels, rows),
        in_specs=[anywhere, vmem, vmem],
        out_specs=[anywhere] * 2,
        out_shape=[jax.ShapeDtypeStruct(temp.shape, f32)] * 2,
        scratch_shapes=[
            pltpu.VMEM((5, stride, columns + SUB, LANES), f32),
            pltpu.VMEM((2, stride, columns, LANES), f32),
            pltpu.VMEM((2, length, width), f32),
            pltpu.VMEM((2, levels, rows, width), f32),
            pltpu.SemaphoreType.DMA((2 * levels,)),
        ]
        + [pltpu.VMEM((nc + 2, stride, SUB, LANES), f32)] * 17
        + [pltpu.VMEM((nc, SUB, LANES), f32)] * 2
        + [pltpu.VMEM((stride, SUB, LANES), f32)] * 2,
        compiler_params=params(40),
    )(turned, from_east, from_west)


def solution(mesh):
    in_specs = (
        P(None, "lat", "lon"),
        P(None, "lat", "lon"),
        P(None, "lat", "lon"),
        P(None, "lat", "lon"),
        P("lat", "lon"),
        P("lat", "lon"),
        P(),
    )
    out_specs = (P(None, "lat", "lon"), P(None, "lat", "lon"))
    body = functools.partial(local, mesh.shape["lon"], mesh.shape["lat"])
    return jax.shard_map(body, mesh=mesh, in_specs=in_specs, out_specs=out_specs, check_vma=False)
```

```python
import functools

import jax
import jax.numpy as jnp
from jax import lax
from jax.experimental import pallas as pl
from jax.experimental.pallas import tpu as pltpu
from jax.sharding import PartitionSpec as P

RATIO_FLOOR = 0.05
DIFFUSIVITY = 0.1
THERMAL_COEF = 0.2
HALINE_COEF = 0.8

BATCH = 3
STEPS = 2
HALO = 4
SUB = 8
LANES = 128


def sublanes():
    return lax.broadcasted_iota(jnp.int32, (SUB, LANES), 0)


def lanes():
    return lax.broadcasted_iota(jnp.int32, (SUB, LANES), 1)


def half_turn(tile):
    return pltpu.roll(tile, 4, 0)


def as_mask(flag):
    return (jnp.zeros((SUB, LANES), jnp.int32) + flag) > 0


def wet_count(indicator, total):
    return jnp.where(indicator == 1, total, 0).astype(jnp.float32)


def pack_rows(levels, width, seam, *refs):
    south, north, (ind_s, ind_n, tot_s, tot_n), (first, second, turn) = refs[:4], refs[4:8], refs[8:12], refs[12:]
    turn[0] = lax.div(seam[0], width)
    lat = lax.axis_index("lat")
    odd = as_mask(lat % 2)
    upper = sublanes() >= HALO
    for i in range(2 * levels):
        f, k = divmod(i, levels)
        low = jnp.where(upper, half_turn(south[f + 2][k]), south[f][k])
        high = jnp.where(upper, north[f][k], half_turn(north[f + 2][k]))
        first[i] = jnp.where(odd, low, high)
        second[i] = jnp.where(odd, high, low)
    low = wet_count(ind_s[...], tot_s[...])
    high = wet_count(ind_n[...], tot_n[...])
    first[2 * levels] = jnp.where(odd, low, high)
    second[2 * levels] = jnp.where(odd, high, low)

    @pl.when(lat == lax.axis_size("lat") - 1)
    def _():
        for i in range(2 * levels):
            f, k = divmod(i, levels)
            for j in range(HALO):
                second[i, j : j + 1, :] = north[f][k, 7 - j : 8 - j, :]
                row = 7 - j if f == 0 else (6, 5, 4, 7)[j]
                second[i, HALO + j : HALO + j + 1, :] = -north[f + 2][k, row : row + 1, :]
        for j in range(HALO):
            second[2 * levels, j : j + 1, :] = wet_count(ind_n[7 - j : 8 - j, :], tot_n[7 - j : 8 - j, :])


def stretch(levels, rows):
    blocks = LANES // levels
    stride = -(-(rows + 2 * HALO) // blocks)
    return blocks, stride, blocks * stride, -(-(HALO + stride * LANES) // SUB) * SUB


def turn_fields(levels, rows, seam, *refs):
    fields, ind, tot, block, q1, q2, q3, turned, to_east, to_west, flat, north_halo, spare = refs[:4], *refs[4:]
    blocks, stride, period, length = stretch(levels, rows)
    half = 2 * levels
    nl = lax.axis_size("lon")
    lat = lax.axis_index("lat")
    odd = as_mask(lat % 2)
    closed = as_mask((lat == 0).astype(jnp.int32))
    lane = lanes()
    upper = sublanes() >= HALO

    def south_halo(i):
        return jnp.where(closed, 0.0, jnp.where(odd, q1[i], q2[i]))

    for i in range(half + 1):
        north_halo[i] = jnp.where(odd, q2[i], q1[i])

    @pl.when(lat == lax.axis_size("lat") - 1)
    def _():
        r = seam[0] & (LANES - 1)
        at_home = lax.rem(lax.div(seam[0], LANES) - 2 * lax.axis_index("lon") + 2 * nl, nl)
        first_own = as_mask((at_home == 0).astype(jnp.int32))
        second_own = as_mask((at_home == 1).astype(jnp.int32))
        for i in range(half + 1):
            at = r - lane - jnp.where(upper, 1 if i < levels else 0, 0)
            index = at & (LANES - 1)

            def pick(tile):
                return jnp.take_along_axis(tile, index, axis=1, mode="promise_in_bounds")

            here = pick(jnp.where(first_own, block[i], q2[i]))
            north_halo[i] = jnp.where(at < 0, pick(jnp.where(second_own, block[i], q3[i])), here)

    tiles = rows // SUB
    for f in range(4):

        def fill(k, carry):
            at = HALO + HALO + k * period
            for t in range(tiles):
                flat[f, pl.ds(at + t * SUB, SUB), :] = fields[f][k, t * SUB : t * SUB + SUB, :]
            i = (f % 2) * levels + k
            n_tile, s_tile = north_halo[i], south_halo(i)
            if f >= 2:
                n_tile, s_tile = half_turn(n_tile), half_turn(s_tile)
            flat[f, pl.ds(at - SUB, SUB), :] = jnp.where(upper, s_tile, 0.0)
            flat[f, pl.ds(at + rows, SUB), :] = jnp.where(upper, 0.0, n_tile)
            return carry

        lax.fori_loop(0, levels, fill, 0, unroll=12)
    for t in range(tiles + 2):
        if t == 0:
            n = jnp.where(upper, south_halo(half), 0.0)
        elif t == tiles + 1:
            n = jnp.where(upper, 0.0, north_halo[half])
        else:
            n = wet_count(ind[t * SUB - SUB : t * SUB, :], tot[t * SUB - SUB : t * SUB, :])

        def left_over(k, carry):
            flat[4, pl.ds(HALO + HALO + k * period + (t - 1) * SUB, SUB), :] = n - k.astype(jnp.float32)
            return carry

        lax.fori_loop(0, levels, left_over, 0, unroll=12)
    end = levels * period
    for f in range(5):
        for t in range(end // SUB * SUB, length, SUB):
            keep = sublanes() + t < end
            flat[f, t : t + SUB, :] = jnp.where(keep, flat[f, t : t + SUB, :], 0.0)

    for t in range(stride):
        for f in range(5):
            turned[f, t] = flat.at[f][pl.ds(HALO + t, LANES, stride=stride), :].T

    places = [(f, t) for f in range(5) for t in range(stride)]
    first = (len(places) + 1) // 2
    for i in range(first):
        f, t = places[i]
        west, east = turned[f, t, 0:SUB, :], turned[f, t, LANES - SUB : LANES, :]
        if i + first < len(places):
            f, t = places[i + first]
            west = jnp.where(upper, half_turn(turned[f, t, 0:SUB, :]), west)
            east = jnp.where(upper, east, half_turn(turned[f, t, LANES - SUB : LANES, :]))
        to_west[i] = west
        to_east[i] = east


def ahead(tiles):
    return tiles[1:] + [pltpu.roll(tiles[0], LANES - 1, 1)]


def behind(tiles):
    return [pltpu.roll(tiles[-1], 1, 1)] + tiles[:-1]


def each(function, *lists):
    return [function(*items) for items in zip(*lists)]


def pairs(function, *lists):
    return tuple(map(list, zip(*each(function, *lists))))


def replaced(tiles, other):
    return [other.get(t, x) for t, x in enumerate(tiles)]


def flux_pair(q, q_next, half_speed, half_size):
    anti = half_size * (q_next - q)
    return half_speed * (q_next + q) - anti, anti


def limited_flux(anti, plus, minus, plus_next, minus_next):
    return anti * jnp.where(anti >= 0.0, jnp.minimum(plus_next, minus), jnp.minimum(plus, minus_next))


def reciprocal(x):
    return pl.reciprocal(x, approx=True)


def halves(speed, mask):
    half = jnp.where(mask > 0.0, 0.5 * speed, 0.0)
    return half, jnp.abs(half)


def net(q, a, b, c, d):
    return q - ((a - b) + (c - d))


def ratios(a, b, c, l, sa, sb, sc, sl):
    inflow = (jnp.maximum(b, 0.0) - jnp.minimum(a, 0.0)) + (jnp.maximum(l, 0.0) - jnp.minimum(c, 0.0))
    outflow = (jnp.maximum(a, 0.0) - jnp.minimum(b, 0.0)) + (jnp.maximum(c, 0.0) - jnp.minimum(l, 0.0))
    rise = jnp.maximum(jnp.maximum(jnp.maximum(sa, sc), 0.0), -jnp.minimum(sb, sl))
    drop = jnp.maximum(jnp.maximum(jnp.maximum(sb, sl), 0.0), -jnp.minimum(sa, sc))
    plus = jnp.minimum(1.0, rise * reciprocal(jnp.maximum(inflow, RATIO_FLOOR)))
    minus = jnp.minimum(1.0, drop * reciprocal(jnp.maximum(outflow, RATIO_FLOOR)))
    return plus, minus


def face(t0, t1, s0, s1, zt0, zt1, zs0, zs1, m):
    dt, ds, zt, zs = t1 - t0, s1 - s0, zt1 + zt0, zs1 + zs0
    bottom = jnp.maximum(HALINE_COEF * zs - THERMAL_COEF * zt, 1.0)
    half_slope = (HALINE_COEF * ds - THERMAL_COEF * dt) * reciprocal(bottom)
    half_slope = jnp.maximum(jnp.minimum(half_slope, 1.0), -1.0)
    return jnp.where(m > 0.0, dt - half_slope * zt, 0.0), jnp.where(m > 0.0, ds - half_slope * zs, 0.0)


class Phases:
    def __init__(self, levels, rows, cell, read, write, alt_read, alt_write):
        blocks, stride, period, length = stretch(levels, rows)
        self.blocks, self.ts, self.nc = blocks, range(stride), LANES // SUB
        self.cell, self.read, self.write = cell, read, write
        self.alt_read, self.alt_write = alt_read, alt_write
        self.held = {}
        self.seam = (rows + HALO - 1) % stride
        self.spare = (rows + 2 * HALO - 1) % stride
        on_top = lax.axis_index("lat") == lax.axis_size("lat") - 1
        tops = as_mask(on_top.astype(jnp.int32))
        self.at_seam = (lanes() % blocks == (rows + HALO - 1) // stride) & tops
        self.first_row, self.last_row = sublanes() == 0, sublanes() == SUB - 1

    def fixed(self, c):
        return c[1] if isinstance(c[0], int) else None

    def load(self, key, c):
        if (key, c[1]) not in self.held:
            fetch = self.cell if isinstance(key, str) else self.read
            self.held[key, c[1]] = [fetch(key, c, t) for t in self.ts]
        return self.held[key, c[1]]

    def following(self, key, c):
        i, nc = self.fixed(c), self.nc
        if i not in (nc - 1, nc):
            return self.load(key, (c[0], c[1] + 1))
        if (key, "next", i) not in self.held:
            own, halo = self.load(key, (0, 0)), self.load(key, (0, nc))
            one, other = (halo, own) if i == nc - 1 else (own, halo)
            self.held[key, "next", i] = [
                pltpu.roll(jnp.where(self.first_row, x, y), SUB - 1, 0) for x, y in zip(one, other)
            ]
        return self.held[key, "next", i]

    def mixed(self, i, last, halo):
        one, other = (halo, last) if i == 0 else (last, halo)
        return [pltpu.roll(jnp.where(self.last_row, x, y), 1, 0) for x, y in zip(one, other)]

    def preceding(self, key, c):
        i, nc = self.fixed(c), self.nc
        if i in (0, nc):
            return self.mixed(i, self.load(key, (0, nc - 1)), self.load(key, (0, nc)))
        return self.load(key, (c[0], c[1] - 1))

    def put(self, place, c, tiles):
        for t in self.ts:
            self.write(place, c, t, tiles[t])

    def upwind_face(self, c):
        m = each(jnp.minimum, self.load("m", c), self.following("m", c))
        speed = pairs(halves, self.load("u", c), m)
        parts = [pairs(flux_pair, self.load(f, c), self.following(f, c), *speed) for f in "TS"]
        self.put(15, c, m)
        for f in range(2):
            self.put(4 + f, c, parts[f][1])
        return [low for low, _ in parts]

    def upwind_cell(self, c, here, before):
        s = self.seam
        m, v = self.load("m", c), self.load("v", c)
        open_a = each(jnp.minimum, m, ahead(m))
        speed = pairs(halves, v, open_a)
        alt = halves(jnp.where(self.at_seam, v[self.spare], v[s]), open_a[s])
        results = []
        for f, key in enumerate("TS"):
            q = self.load(key, c)
            q_a = ahead(q)
            low_a, anti_a = pairs(flux_pair, q, q_a, *speed)
            low_alt, anti_alt = flux_pair(q[s], q_a[s], *alt)
            low_b = behind(replaced(low_a, {s: low_alt}))
            results.append((each(net, q, low_a, low_b, here[f], before[f]), anti_a, anti_alt))
        self.put(14, c, open_a)
        self.put(16, c, m)
        for f, (upwind, anti_a, anti_alt) in enumerate(results):
            self.put(f, c, upwind)
            self.put(2 + f, c, anti_a)
            self.alt_write(f, c, anti_alt)

    def ratio_face(self, c):
        m = self.load(15, c)
        return [
            each(lambda x, n, o: jnp.where(o > 0.0, n - x, 0.0), self.load(f, c), self.following(f, c), m)
            for f in range(2)
        ]

    def ratio_cell(self, c, here, before):
        open_a = self.load(14, c)
        results = []
        for f in range(2):
            up, anti_a = self.load(f, c), self.load(2 + f, c)
            step_a = each(lambda x, n, o: jnp.where(o > 0.0, n - x, 0.0), up, ahead(up), open_a)
            anti_b = behind(replaced(anti_a, {self.seam: self.alt_read(f, c)}))
            anti_c, anti_l = self.load(4 + f, c), self.preceding(4 + f, c)
            results.append(
                pairs(ratios, anti_a, anti_b, anti_c, anti_l, step_a, behind(step_a), here[f], before[f])
            )
        for f, (plus, minus) in enumerate(results):
            self.put(6 + f, c, plus)
            self.put(8 + f, c, minus)

    def limited_face(self, c):
        return [
            each(
                limited_flux, self.load(4 + f, c), self.load(6 + f, c), self.load(8 + f, c),
                self.following(6 + f, c), self.following(8 + f, c),
            )
            for f in range(2)
        ]

    def limited_cell(self, c, here, before):
        s, m = self.seam, self.load(16, c)
        results = []
        for f in range(2):
            plus, minus = self.load(6 + f, c), self.load(8 + f, c)
            plus_a, minus_a = ahead(plus), ahead(minus)
            lim_a = each(limited_flux, self.load(2 + f, c), plus, minus, plus_a, minus_a)
            lim_alt = limited_flux(self.alt_read(f, c), plus[s], minus[s], plus_a[s], minus_a[s])
            lim_b = behind(replaced(lim_a, {s: lim_alt}))
            new = each(net, self.load(f, c), lim_a, lim_b, here[f], before[f])
            results.append(
                (new, each(lambda x, n: jnp.where(n > 1.0, pltpu.roll(x, LANES - self.blocks, 1) - x, 0.0), new, m))
            )
        for f, (new, below) in enumerate(results):
            self.put(10 + f, c, new)
            self.put(12 + f, c, below)

    def diffuse_face(self, c):
        sides = [side for p in (10, 11, 12, 13) for side in (self.load(p, c), self.following(p, c))]
        return list(pairs(face, *sides, self.load(15, c)))

    def diffuse_cell(self, c, here, before):
        values = [self.load(p, c) for p in (10, 11, 12, 13)]
        along = pairs(face, *[side for x in values for side in (x, ahead(x))], self.load(14, c))
        for f in range(2):
            new = each(
                lambda q, a, b, x, y: q + DIFFUSIVITY * ((a - b) + (x - y)),
                values[f], along[f], behind(along[f]), here[f], before[f],
            )
            self.put(17 + f, c, new)

    def all(self):
        return (
            (self.upwind_face, self.upwind_cell),
            (self.ratio_face, self.ratio_cell),
            (self.limited_face, self.limited_cell),
            (self.diffuse_face, self.diffuse_cell),
        )


FIELDS = "TSuvm"


def inner_step(levels, rows, turned, *refs):
    grid, alts, prev = refs[:19], refs[19:21], refs[21:]

    def cell(key, c, t):
        return turned.at[FIELDS.index(key), t][pl.ds(sum(c), SUB, stride=LANES // SUB), :]

    def read(place, c, t):
        return grid[place][sum(c), t]

    def write(place, c, t, tile):
        grid[place][sum(c), t] = tile

    def alt_read(f, c):
        return alts[f][sum(c)]

    def alt_write(f, c, tile):
        alts[f][sum(c)] = tile

    phases = Phases(levels, rows, cell, read, write, alt_read, alt_write)
    ts = phases.ts

    def store(lists):
        for ref, tiles in zip(prev, lists):
            for t in ts:
                ref[t] = tiles[t]

    for i, (make_face, make_cell) in enumerate(phases.all()):
        low, high = i + 1, phases.nc - 1 - i
        count = (high - low) // STEPS
        phases.held.clear()
        store(make_face((0, low - 1)))

        def some(g, carry):
            start = low + g * count
            phases.held.clear()
            before = [[ref[t] for t in ts] for ref in prev]
            for n in range(count):
                here = make_face((start, n))
                make_cell((start, n), here, before)
                before = here
            store(before)
            phases.held.clear()
            return carry

        lax.fori_loop(0, STEPS, some, 0)


def outer_step(levels, rows, turned, from_east, from_west, *refs):
    inner, inner_alts, (temp_out, salt_out), refs = refs[:19], refs[19:21], refs[21:23], refs[23:]
    grid, alts, result, flat, out, sems = refs[:17], refs[17:19], *refs[19:]
    blocks, stride, period, length = stretch(levels, rows)
    ts = range(stride)
    upper = sublanes() >= HALO
    first = (5 * stride + 1) // 2
    nc = LANES // SUB
    made = [set() for _ in range(17)]
    made_alts = set()

    def slot(c):
        return (sum(c) + HALO) % (nc + 1)

    def cell(key, c, t):
        f = FIELDS.index(key)
        if sum(c) < nc:
            return turned.at[f, t][pl.ds(sum(c), SUB, stride=nc), :]
        i = f * stride + t
        if i < first:
            return jnp.where(upper, from_west[i], from_east[i])
        return half_turn(jnp.where(upper, from_east[i - first], from_west[i - first]))

    def read(place, c, t):
        return grid[place][slot(c), t] if sum(c) in made[place] else inner[place][sum(c), t]

    def write(place, c, t, tile):
        if place < 17:
            made[place].add(sum(c))
            grid[place][slot(c), t] = tile
        elif sum(c) < nc:
            result.at[place - 17, t][pl.ds(sum(c), SUB, stride=nc), :] = tile

    def alt_read(f, c):
        return alts[f][slot(c)] if sum(c) in made_alts else inner_alts[f][sum(c)]

    def alt_write(f, c, tile):
        made_alts.add(sum(c))
        alts[f][slot(c)] = tile

    phases = Phases(levels, rows, cell, read, write, alt_read, alt_write)
    for i, (make_face, make_cell) in enumerate(phases.all()):
        columns = [*range(nc - 1 - i, nc + 1), *range(i + 1)]
        phases.held.clear()
        faces = {c: make_face((0, c)) for c in [columns[0] - 1] + columns}
        for c in columns:
            if c == nc and i == 3:
                continue
            if c in (0, nc):
                before = each(lambda x, h: phases.mixed(c, x, h), faces[nc - 1], faces[nc])
            else:
                before = faces[c - 1]
            make_cell((0, c), faces[c], before)
    for f in range(2):
        for c in range(4, nc - 4):
            for t in ts:
                result.at[f, t][pl.ds(c, SUB, stride=nc), :] = inner[17 + f][c, t]

    stores = []
    for f, ref in enumerate((temp_out, salt_out)):
        for t in ts:
            flat.at[f][pl.ds(HALO + t, LANES, stride=stride), :] = result[f, t].T
        for g in range(0, levels, BATCH):
            for k in range(g, g + BATCH):
                for t in range(rows // SUB):
                    at = HALO + HALO + k * period + t * SUB
                    out[f, k, t * SUB : t * SUB + SUB, :] = flat[f, at : at + SUB, :]
            levels_of = pl.ds(g, BATCH)
            store = pltpu.make_async_copy(out.at[f, levels_of], ref.at[levels_of], sems.at[len(stores)])
            store.start()
            stores.append(store)
    for store in stores:
        store.wait()


def local(nl, nlat, temp, salt, east, north, indicator, total, seam):
    levels, rows, width = temp.shape
    half = 2 * levels
    blocks, stride, period, length = stretch(levels, rows)
    vmem = pl.BlockSpec(memory_space=pltpu.VMEM)
    smem = pl.BlockSpec(memory_space=pltpu.SMEM)
    anywhere = pl.BlockSpec(memory_space=pl.ANY)
    f32 = jnp.float32

    def params(mib):
        return pltpu.CompilerParams(vmem_limit_bytes=mib * 1024 * 1024)

    last = rows // SUB - 1
    low = pl.BlockSpec((levels, SUB, width), lambda i: (0, 0, 0))
    high = pl.BlockSpec((levels, SUB, width), lambda i: (0, last, 0))
    flat_low = pl.BlockSpec((SUB, width), lambda i: (0, 0))
    flat_high = pl.BlockSpec((SUB, width), lambda i: (last, 0))
    block = jax.ShapeDtypeStruct((half + 1, SUB, width), f32)
    whole_block = pl.BlockSpec((half + 1, SUB, width), lambda i: (0, 0, 0))
    fields = (temp, salt, east, north)
    first, second, turn = pl.pallas_call(
        functools.partial(pack_rows, levels, width),
        grid=(1,),
        in_specs=[smem] + [low] * 4 + [high] * 4 + [flat_low, flat_high] * 2,
        out_specs=[whole_block] * 2 + [smem],
        out_shape=[block] * 2 + [jax.ShapeDtypeStruct((1,), jnp.int32)],
        compiler_params=params(56),
    )(seam, *fields, *fields, indicator, indicator, total, total)

    q1 = lax.ppermute(first, "lat", [(j, j ^ 1) for j in range(nlat)])

    def meet(turned):
        def facing(back):
            pairs = []
            for i in range(nl):
                to = (turned - back - i) % nl
                to = (i + nl // 2) % nl if to == i else to
                pairs.append((i * nlat + nlat - 1, to * nlat + nlat - 1))
            return pairs

        def idle(rows):
            return [(i * nlat + j, (i ^ 1) * nlat + j) for i in range(nl) for j in rows]

        inner = [(i * nlat + j, i * nlat + (j + 1 if j % 2 else j - 1)) for i in range(nl) for j in range(1, nlat - 1)]

        def send(x):
            return (
                lax.ppermute(x, ("lon", "lat"), idle([0]) + inner + facing(0)),
                lax.ppermute(x, ("lon", "lat"), idle(range(nlat - 1)) + facing(1)),
            )

        return send

    q2, q3 = lax.switch(turn[0], [meet(t) for t in range(nl)], second)

    payload = jax.ShapeDtypeStruct(((5 * stride + 1) // 2, SUB, width), f32)
    turned, to_east, to_west = pl.pallas_call(
        functools.partial(turn_fields, levels, rows),
        in_specs=[smem] + [vmem] * 10,
        out_specs=[vmem] * 3,
        out_shape=[jax.ShapeDtypeStruct((5, stride, width, LANES), f32), payload, payload],
        scratch_shapes=[
            pltpu.VMEM((5, length, width), f32),
            pltpu.VMEM((half + 1, SUB, width), f32),
            pltpu.VMEM((SUB, width), f32),
        ],
        compiler_params=params(20),
    )(seam, *fields, indicator, total, second, q1, q2, q3)
    from_west = lax.ppermute(to_east, "lon", [(i, (i + 1) % nl) for i in range(nl)])
    from_east = lax.ppermute(to_west, "lon", [((i + 1) % nl, i) for i in range(nl)])

    nc = width // SUB
    column = jax.ShapeDtypeStruct((nc + 1, stride, SUB, LANES), f32)
    single = jax.ShapeDtypeStruct((nc + 1, SUB, LANES), f32)
    inner = pl.pallas_call(
        functools.partial(inner_step, levels, rows),
        in_specs=[vmem],
        out_specs=[vmem] * 21,
        out_shape=[column] * 19 + [single] * 2,
        scratch_shapes=[pltpu.VMEM((stride, SUB, LANES), f32)] * 2,
        compiler_params=params(24),
        cost_estimate=pl.CostEstimate(flops=20_000_000, bytes_accessed=10_000_000, transcendentals=0),
    )(turned)
    return pl.pallas_call(
        functools.partial(outer_step, levels, rows),
        in_specs=[vmem] * 24,
        out_specs=[anywhere] * 2,
        out_shape=[jax.ShapeDtypeStruct(temp.shape, f32)] * 2,
        scratch_shapes=[pltpu.VMEM((2 * HALO, stride, SUB, LANES), f32)] * 17
        + [pltpu.VMEM((2 * HALO, SUB, LANES), f32)] * 2
        + [
            pltpu.VMEM((2, stride, width, LANES), f32),
            pltpu.VMEM((2, length, width), f32),
            pltpu.VMEM((2, levels, rows, width), f32),
            pltpu.SemaphoreType.DMA((2 * levels,)),
        ],
        compiler_params=params(32),
    )(turned, from_east, from_west, *inner)


def solution(mesh):
    in_specs = (
        P(None, "lat", "lon"),
        P(None, "lat", "lon"),
        P(None, "lat", "lon"),
        P(None, "lat", "lon"),
        P("lat", "lon"),
        P("lat", "lon"),
        P(),
    )
    out_specs = (P(None, "lat", "lon"), P(None, "lat", "lon"))
    body = functools.partial(local, mesh.shape["lon"], mesh.shape["lat"])
    return jax.shard_map(body, mesh=mesh, in_specs=in_specs, out_specs=out_specs, check_vma=False)
```

```python
import functools

import jax
import jax.numpy as jnp
from jax import lax
from jax.experimental import pallas as pl
from jax.experimental.pallas import tpu as pltpu
from jax.sharding import PartitionSpec as P

RATIO_FLOOR = 0.05
DIFFUSIVITY = 0.1
THERMAL_COEF = 0.2
HALINE_COEF = 0.8

BATCH = 3
STEPS = 1
HALO = 4
SUB = 8
LANES = 128
PADDED = LANES + LANES // SUB


def sublanes():
    return lax.broadcasted_iota(jnp.int32, (SUB, LANES), 0)


def lanes():
    return lax.broadcasted_iota(jnp.int32, (SUB, LANES), 1)


def half_turn(tile):
    return pltpu.roll(tile, 4, 0)


def as_mask(flag):
    return (jnp.zeros((SUB, LANES), jnp.int32) + flag) > 0


def wet_count(indicator, total):
    return jnp.where(indicator == 1, total, 0).astype(jnp.float32)


def fold_half(seam):
    return (2 * (seam[0] & (LANES - 1)) < LANES).astype(jnp.int32)


def pack_rows(levels, width, seam, *refs):
    south, north, (ind_s, ind_n, tot_s, tot_n), (first, second, third, turn) = refs[:4], refs[4:8], refs[8:12], refs[12:]
    low_half = fold_half(seam)
    turn[0] = 2 * lax.div(seam[0], width) + low_half
    lat = lax.axis_index("lat")
    odd = as_mask(lat % 2)
    upper = sublanes() >= HALO
    for i in range(2 * levels):
        f, k = divmod(i, levels)
        low = jnp.where(upper, half_turn(south[f + 2][k]), south[f][k])
        high = jnp.where(upper, north[f][k], half_turn(north[f + 2][k]))
        first[i] = jnp.where(odd, low, high)
        second[i] = jnp.where(odd, high, low)
    low = wet_count(ind_s[...], tot_s[...])
    high = wet_count(ind_n[...], tot_n[...])
    first[2 * levels] = jnp.where(odd, low, high)
    second[2 * levels] = jnp.where(odd, high, low)

    for i in range(levels + 1):
        third[i] = jnp.zeros((SUB, LANES), jnp.float32)

    @pl.when(lat == lax.axis_size("lat") - 1)
    def _():
        for i in range(2 * levels):
            f, k = divmod(i, levels)
            for j in range(HALO):
                second[i, j : j + 1, :] = north[f][k, 7 - j : 8 - j, :]
                row = 7 - j if f == 0 else (6, 5, 4, 7)[j]
                second[i, HALO + j : HALO + j + 1, :] = -north[f + 2][k, row : row + 1, :]
        for j in range(HALO):
            second[2 * levels, j : j + 1, :] = wet_count(ind_n[7 - j : 8 - j, :], tot_n[7 - j : 8 - j, :])
        low = as_mask(low_half)
        for i in range(levels + 1):
            even = second[2 * i]
            odd_one = second[min(2 * i + 1, 2 * levels)]
            left = jnp.where(low, even, pltpu.roll(even, LANES // 2, 1))
            right = jnp.where(low, pltpu.roll(odd_one, LANES // 2, 1), odd_one)
            third[i] = jnp.where(lanes() < LANES // 2, left, right)


def stretch(levels, rows):
    blocks = LANES // levels
    stride = -(-(rows + 2 * HALO) // blocks)
    return blocks, stride, blocks * stride, -(-(HALO + stride * (LANES + 1)) // SUB) * SUB


def turn_fields(levels, rows, seam, *refs):
    fields, ind, tot, block, half_block, q1, q2, q3, turned, to_east, to_west, flat, north_halo, spare = refs[:4], *refs[4:]
    blocks, stride, period, length = stretch(levels, rows)
    half = 2 * levels
    nl = lax.axis_size("lon")
    lat = lax.axis_index("lat")
    odd = as_mask(lat % 2)
    closed = as_mask((lat == 0).astype(jnp.int32))
    lane = lanes()
    upper = sublanes() >= HALO

    def south_halo(i):
        return jnp.where(closed, 0.0, jnp.where(odd, q1[i], q2[i]))

    for i in range(half + 1):
        north_halo[i] = jnp.where(odd, q2[i], q1[i])

    @pl.when(lat == lax.axis_size("lat") - 1)
    def _():
        r = seam[0] & (LANES - 1)
        low = fold_half(seam)
        home = lax.div(seam[0], LANES) - 2 * lax.axis_index("lon") + 2 * nl
        whole_own = as_mask((lax.rem(home - low, nl) == 0).astype(jnp.int32))
        half_own = as_mask((lax.rem(home - 1 + low, nl) == 0).astype(jnp.int32))
        for i in range(half + 1):
            at = r - lane - jnp.where(upper, 1 if i < levels else 0, 0)

            def pick(tile, column):
                return jnp.take_along_axis(tile, column & (LANES - 1), axis=1, mode="promise_in_bounds")

            whole = pick(jnp.where(whole_own, block[i], q2[i]), at)
            offset = LANES // 2 * (1 - low + i % 2)
            part = pick(jnp.where(half_own, half_block[i // 2], q3[i // 2]), at + offset)
            north_halo[i] = jnp.where((1 - 2 * low) * at >= low, whole, part)

    tiles = rows // SUB
    for f in range(4):

        def fill(k, carry):
            at = HALO + HALO + k * period
            for t in range(tiles):
                flat[f, pl.ds(at + t * SUB, SUB), :] = fields[f][k, t * SUB : t * SUB + SUB, :]
            i = (f % 2) * levels + k
            n_tile, s_tile = north_halo[i], south_halo(i)
            if f >= 2:
                n_tile, s_tile = half_turn(n_tile), half_turn(s_tile)
            flat[f, pl.ds(at - SUB, SUB), :] = jnp.where(upper, s_tile, 0.0)
            flat[f, pl.ds(at + rows, SUB), :] = jnp.where(upper, 0.0, n_tile)
            return carry

        lax.fori_loop(0, levels, fill, 0, unroll=12)
    for t in range(tiles + 2):
        if t == 0:
            n = jnp.where(upper, south_halo(half), 0.0)
        elif t == tiles + 1:
            n = jnp.where(upper, 0.0, north_halo[half])
        else:
            n = wet_count(ind[t * SUB - SUB : t * SUB, :], tot[t * SUB - SUB : t * SUB, :])

        def left_over(k, carry):
            flat[4, pl.ds(HALO + HALO + k * period + (t - 1) * SUB, SUB), :] = n - k.astype(jnp.float32)
            return carry

        lax.fori_loop(0, levels, left_over, 0, unroll=12)
    end = levels * period
    for f in range(5):
        for t in range(end // SUB * SUB, length, SUB):
            keep = sublanes() + t < end
            flat[f, t : t + SUB, :] = jnp.where(keep, flat[f, t : t + SUB, :], 0.0)

    for t in range(stride):
        for f in range(5):
            turned[f, t, 0:LANES, :] = flat.at[f][pl.ds(HALO + t, LANES, stride=stride), :].T

    places = [(f, t) for f in range(5) for t in range(stride)]
    first = (len(places) + 1) // 2
    for i in range(first):
        f, t = places[i]
        west, east = turned[f, t, 0:SUB, :], turned[f, t, LANES - SUB : LANES, :]
        if i + first < len(places):
            f, t = places[i + first]
            west = jnp.where(upper, half_turn(turned[f, t, 0:SUB, :]), west)
            east = jnp.where(upper, east, half_turn(turned[f, t, LANES - SUB : LANES, :]))
        to_west[i] = west
        to_east[i] = east


def ahead(tiles):
    return tiles[1:] + [pltpu.roll(tiles[0], LANES - 1, 1)]


def behind(tiles):
    return [pltpu.roll(tiles[-1], 1, 1)] + tiles[:-1]


def each(function, *lists):
    return [function(*items) for items in zip(*lists)]


def pairs(function, *lists):
    return tuple(map(list, zip(*each(function, *lists))))


def replaced(tiles, other):
    return [other.get(t, x) for t, x in enumerate(tiles)]


def flux_pair(q, q_next, half_speed, half_size):
    anti = half_size * (q_next - q)
    return half_speed * (q_next + q) - anti, anti


def limited_flux(anti, plus, minus, plus_next, minus_next):
    return anti * jnp.where(anti >= 0.0, jnp.minimum(plus_next, minus), jnp.minimum(plus, minus_next))


def reciprocal(x):
    return pl.reciprocal(x, approx=True)


def halves(speed, mask):
    half = jnp.where(mask > 0.0, 0.5 * speed, 0.0)
    return half, jnp.abs(half)


def net(q, a, b, c, d):
    return q - ((a - b) + (c - d))


def ratios(a, b, c, l, sa, sb, sc, sl):
    inflow = (jnp.maximum(b, 0.0) - jnp.minimum(a, 0.0)) + (jnp.maximum(l, 0.0) - jnp.minimum(c, 0.0))
    outflow = (jnp.maximum(a, 0.0) - jnp.minimum(b, 0.0)) + (jnp.maximum(c, 0.0) - jnp.minimum(l, 0.0))
    rise = jnp.maximum(jnp.maximum(jnp.maximum(sa, sc), 0.0), -jnp.minimum(sb, sl))
    drop = jnp.maximum(jnp.maximum(jnp.maximum(sb, sl), 0.0), -jnp.minimum(sa, sc))
    plus = jnp.minimum(1.0, rise * reciprocal(jnp.maximum(inflow, RATIO_FLOOR)))
    minus = jnp.minimum(1.0, drop * reciprocal(jnp.maximum(outflow, RATIO_FLOOR)))
    return plus, minus


def face(t0, t1, s0, s1, zt0, zt1, zs0, zs1, m):
    dt, ds, zt, zs = t1 - t0, s1 - s0, zt1 + zt0, zs1 + zs0
    bottom = jnp.maximum(HALINE_COEF * zs - THERMAL_COEF * zt, 1.0)
    half_slope = (HALINE_COEF * ds - THERMAL_COEF * dt) * reciprocal(bottom)
    half_slope = jnp.maximum(jnp.minimum(half_slope, 1.0), -1.0)
    return jnp.where(m > 0.0, dt - half_slope * zt, 0.0), jnp.where(m > 0.0, ds - half_slope * zs, 0.0)


class Phases:
    def __init__(self, levels, rows, cell, read, write, alt_read, alt_write):
        blocks, stride, period, length = stretch(levels, rows)
        self.blocks, self.ts, self.nc = blocks, range(stride), LANES // SUB
        self.cell, self.read, self.write = cell, read, write
        self.alt_read, self.alt_write = alt_read, alt_write
        self.held = {}
        self.seam = (rows + HALO - 1) % stride
        self.spare = (rows + 2 * HALO - 1) % stride
        on_top = lax.axis_index("lat") == lax.axis_size("lat") - 1
        tops = as_mask(on_top.astype(jnp.int32))
        self.at_seam = (lanes() % blocks == (rows + HALO - 1) // stride) & tops
        self.first_row, self.last_row = sublanes() == 0, sublanes() == SUB - 1

    def fixed(self, c):
        return c[1] if isinstance(c[0], int) else None

    def load(self, key, c):
        if (key, c[1]) not in self.held:
            fetch = self.cell if isinstance(key, str) else self.read
            self.held[key, c[1]] = [fetch(key, c, t) for t in self.ts]
        return self.held[key, c[1]]

    def following(self, key, c):
        i, nc = self.fixed(c), self.nc
        if i not in (nc - 1, nc):
            return self.load(key, (c[0], c[1] + 1))
        if (key, "next", i) not in self.held:
            own, halo = self.load(key, (0, 0)), self.load(key, (0, nc))
            one, other = (halo, own) if i == nc - 1 else (own, halo)
            self.held[key, "next", i] = [
                pltpu.roll(jnp.where(self.first_row, x, y), SUB - 1, 0) for x, y in zip(one, other)
            ]
        return self.held[key, "next", i]

    def mixed(self, i, last, halo):
        one, other = (halo, last) if i == 0 else (last, halo)
        return [pltpu.roll(jnp.where(self.last_row, x, y), 1, 0) for x, y in zip(one, other)]

    def preceding(self, key, c):
        i, nc = self.fixed(c), self.nc
        if i in (0, nc):
            return self.mixed(i, self.load(key, (0, nc - 1)), self.load(key, (0, nc)))
        return self.load(key, (c[0], c[1] - 1))

    def put(self, place, c, tiles):
        for t in self.ts:
            self.write(place, c, t, tiles[t])

    def upwind_face(self, c):
        m = each(jnp.minimum, self.load("m", c), self.following("m", c))
        speed = pairs(halves, self.load("u", c), m)
        parts = [pairs(flux_pair, self.load(f, c), self.following(f, c), *speed) for f in "TS"]
        self.put(15, c, m)
        for f in range(2):
            self.put(4 + f, c, parts[f][1])
        return [low for low, _ in parts]

    def upwind_cell(self, c, here, before):
        s = self.seam
        m, v = self.load("m", c), self.load("v", c)
        open_a = each(jnp.minimum, m, ahead(m))
        speed = pairs(halves, v, open_a)
        alt = halves(jnp.where(self.at_seam, v[self.spare], v[s]), open_a[s])
        results = []
        for f, key in enumerate("TS"):
            q = self.load(key, c)
            q_a = ahead(q)
            low_a, anti_a = pairs(flux_pair, q, q_a, *speed)
            low_alt, anti_alt = flux_pair(q[s], q_a[s], *alt)
            low_b = behind(replaced(low_a, {s: low_alt}))
            results.append((each(net, q, low_a, low_b, here[f], before[f]), anti_a, anti_alt))
        self.put(14, c, open_a)
        self.put(16, c, m)
        for f, (upwind, anti_a, anti_alt) in enumerate(results):
            self.put(f, c, upwind)
            self.put(2 + f, c, anti_a)
            self.alt_write(f, c, anti_alt)

    def ratio_face(self, c):
        m = self.load(15, c)
        return [
            each(lambda x, n, o: jnp.where(o > 0.0, n - x, 0.0), self.load(f, c), self.following(f, c), m)
            for f in range(2)
        ]

    def ratio_cell(self, c, here, before):
        open_a = self.load(14, c)
        results = []
        for f in range(2):
            up, anti_a = self.load(f, c), self.load(2 + f, c)
            step_a = each(lambda x, n, o: jnp.where(o > 0.0, n - x, 0.0), up, ahead(up), open_a)
            anti_b = behind(replaced(anti_a, {self.seam: self.alt_read(f, c)}))
            anti_c, anti_l = self.load(4 + f, c), self.preceding(4 + f, c)
            results.append(
                pairs(ratios, anti_a, anti_b, anti_c, anti_l, step_a, behind(step_a), here[f], before[f])
            )
        for f, (plus, minus) in enumerate(results):
            self.put(6 + f, c, plus)
            self.put(8 + f, c, minus)

    def limited_face(self, c):
        return [
            each(
                limited_flux, self.load(4 + f, c), self.load(6 + f, c), self.load(8 + f, c),
                self.following(6 + f, c), self.following(8 + f, c),
            )
            for f in range(2)
        ]

    def limited_cell(self, c, here, before):
        s, m = self.seam, self.load(16, c)
        results = []
        for f in range(2):
            plus, minus = self.load(6 + f, c), self.load(8 + f, c)
            plus_a, minus_a = ahead(plus), ahead(minus)
            lim_a = each(limited_flux, self.load(2 + f, c), plus, minus, plus_a, minus_a)
            lim_alt = limited_flux(self.alt_read(f, c), plus[s], minus[s], plus_a[s], minus_a[s])
            lim_b = behind(replaced(lim_a, {s: lim_alt}))
            new = each(net, self.load(f, c), lim_a, lim_b, here[f], before[f])
            results.append(
                (new, each(lambda x, n: jnp.where(n > 1.0, pltpu.roll(x, LANES - self.blocks, 1) - x, 0.0), new, m))
            )
        for f, (new, below) in enumerate(results):
            self.put(10 + f, c, new)
            self.put(12 + f, c, below)

    def diffuse_face(self, c):
        sides = [side for p in (10, 11, 12, 13) for side in (self.load(p, c), self.following(p, c))]
        return list(pairs(face, *sides, self.load(15, c)))

    def diffuse_cell(self, c, here, before):
        values = [self.load(p, c) for p in (10, 11, 12, 13)]
        along = pairs(face, *[side for x in values for side in (x, ahead(x))], self.load(14, c))
        for f in range(2):
            new = each(
                lambda q, a, b, x, y: q + DIFFUSIVITY * ((a - b) + (x - y)),
                values[f], along[f], behind(along[f]), here[f], before[f],
            )
            self.put(17 + f, c, new)

    def all(self):
        return (
            (self.upwind_face, self.upwind_cell),
            (self.ratio_face, self.ratio_cell),
            (self.limited_face, self.limited_cell),
            (self.diffuse_face, self.diffuse_cell),
        )


FIELDS = "TSuvm"


def inner_step(levels, rows, turned, *refs):
    grid, alts, prev = refs[:19], refs[19:21], refs[21:]

    def cell(key, c, t):
        return turned.at[FIELDS.index(key), t][pl.ds(sum(c), SUB, stride=LANES // SUB), :]

    def read(place, c, t):
        return grid[place][sum(c), t]

    def write(place, c, t, tile):
        grid[place][sum(c), t] = tile

    def alt_read(f, c):
        return alts[f][sum(c)]

    def alt_write(f, c, tile):
        alts[f][sum(c)] = tile

    phases = Phases(levels, rows, cell, read, write, alt_read, alt_write)
    ts = phases.ts

    def store(lists):
        for ref, tiles in zip(prev, lists):
            for t in ts:
                ref[t] = tiles[t]

    for i, (make_face, make_cell) in enumerate(phases.all()):
        low, high = i + 1, phases.nc - 1 - i
        count = (high - low) // STEPS
        phases.held.clear()
        store(make_face((0, low - 1)))

        def some(g, carry):
            start = low + g * count
            phases.held.clear()
            before = [[ref[t] for t in ts] for ref in prev]
            for n in range(count):
                here = make_face((start, n))
                make_cell((start, n), here, before)
                before = here
            store(before)
            phases.held.clear()
            return carry

        lax.fori_loop(0, STEPS, some, 0)


def outer_step(levels, rows, turned, from_east, from_west, *refs):
    inner, inner_alts, (temp_out, salt_out), refs = refs[:19], refs[19:21], refs[21:23], refs[23:]
    grid, alts, result, flat, out, sems = refs[:17], refs[17:19], *refs[19:]
    blocks, stride, period, length = stretch(levels, rows)
    ts = range(stride)
    upper = sublanes() >= HALO
    first = (5 * stride + 1) // 2
    nc = LANES // SUB
    made = [set() for _ in range(17)]
    made_alts = set()

    def slot(c):
        return (sum(c) + HALO) % (nc + 1)

    def cell(key, c, t):
        f = FIELDS.index(key)
        if sum(c) < nc:
            return turned.at[f, t][pl.ds(sum(c), SUB, stride=nc), :]
        i = f * stride + t
        if i < first:
            return jnp.where(upper, from_west[i], from_east[i])
        return half_turn(jnp.where(upper, from_east[i - first], from_west[i - first]))

    def read(place, c, t):
        return grid[place][slot(c), t] if sum(c) in made[place] else inner[place][sum(c), t]

    def write(place, c, t, tile):
        if place < 17:
            made[place].add(sum(c))
            grid[place][slot(c), t] = tile
        elif sum(c) < nc:
            result.at[place - 17, t][pl.ds(sum(c), SUB, stride=nc), :] = tile

    def alt_read(f, c):
        return alts[f][slot(c)] if sum(c) in made_alts else inner_alts[f][sum(c)]

    def alt_write(f, c, tile):
        made_alts.add(sum(c))
        alts[f][slot(c)] = tile

    phases = Phases(levels, rows, cell, read, write, alt_read, alt_write)
    for i, (make_face, make_cell) in enumerate(phases.all()):
        columns = [*range(nc - 1 - i, nc + 1), *range(i + 1)]
        phases.held.clear()
        faces = {c: make_face((0, c)) for c in [columns[0] - 1] + columns}
        for c in columns:
            if c == nc and i == 3:
                continue
            if c in (0, nc):
                before = each(lambda x, h: phases.mixed(c, x, h), faces[nc - 1], faces[nc])
            else:
                before = faces[c - 1]
            make_cell((0, c), faces[c], before)
    for f in range(2):
        for c in range(4, nc - 4):
            for t in ts:
                result.at[f, t][pl.ds(c, SUB, stride=nc), :] = inner[17 + f][c, t]

    stores = []
    for f, ref in enumerate((temp_out, salt_out)):
        for t in ts:
            flat.at[f][pl.ds(HALO + t, LANES, stride=stride), :] = result[f, t, 0:LANES, :].T
        for g in range(0, levels, BATCH):
            for k in range(g, g + BATCH):
                for t in range(rows // SUB):
                    at = HALO + HALO + k * period + t * SUB
                    out[f, k, t * SUB : t * SUB + SUB, :] = flat[f, at : at + SUB, :]
            levels_of = pl.ds(g, BATCH)
            store = pltpu.make_async_copy(out.at[f, levels_of], ref.at[levels_of], sems.at[len(stores)])
            store.start()
            stores.append(store)
    for store in stores:
        store.wait()


def local(nl, nlat, temp, salt, east, north, indicator, total, seam):
    levels, rows, width = temp.shape
    half = 2 * levels
    blocks, stride, period, length = stretch(levels, rows)
    vmem = pl.BlockSpec(memory_space=pltpu.VMEM)
    smem = pl.BlockSpec(memory_space=pltpu.SMEM)
    anywhere = pl.BlockSpec(memory_space=pl.ANY)
    f32 = jnp.float32

    def params(mib):
        return pltpu.CompilerParams(vmem_limit_bytes=mib * 1024 * 1024)

    last = rows // SUB - 1
    low = pl.BlockSpec((levels, SUB, width), lambda i: (0, 0, 0))
    high = pl.BlockSpec((levels, SUB, width), lambda i: (0, last, 0))
    flat_low = pl.BlockSpec((SUB, width), lambda i: (0, 0))
    flat_high = pl.BlockSpec((SUB, width), lambda i: (last, 0))
    block = jax.ShapeDtypeStruct((half + 1, SUB, width), f32)
    whole_block = pl.BlockSpec((half + 1, SUB, width), lambda i: (0, 0, 0))
    fields = (temp, salt, east, north)
    halves_block = jax.ShapeDtypeStruct((levels + 1, SUB, width), f32)
    whole_halves = pl.BlockSpec((levels + 1, SUB, width), lambda i: (0, 0, 0))
    first, second, third, turn = pl.pallas_call(
        functools.partial(pack_rows, levels, width),
        grid=(1,),
        in_specs=[smem] + [low] * 4 + [high] * 4 + [flat_low, flat_high] * 2,
        out_specs=[whole_block] * 2 + [whole_halves, smem],
        out_shape=[block] * 2 + [halves_block, jax.ShapeDtypeStruct((1,), jnp.int32)],
        compiler_params=params(56),
    )(seam, *fields, *fields, indicator, indicator, total, total)

    q1 = lax.ppermute(first, "lat", [(j, j ^ 1) for j in range(nlat)])

    def meet(index):
        back, low = divmod(index, 2)

        def facing(back):
            pairs = []
            for i in range(nl):
                to = (back - i) % nl
                to = (i + nl // 2) % nl if to == i else to
                pairs.append((i * nlat + nlat - 1, to * nlat + nlat - 1))
            return pairs

        def idle(rows):
            return [(i * nlat + j, (i ^ 1) * nlat + j) for i in range(nl) for j in rows]

        inner = [(i * nlat + j, i * nlat + (j + 1 if j % 2 else j - 1)) for i in range(nl) for j in range(1, nlat - 1)]

        def send(x, y):
            return (
                lax.ppermute(x, ("lon", "lat"), idle([0]) + inner + facing(back - low)),
                lax.ppermute(y, ("lon", "lat"), idle(range(nlat - 1)) + facing(back - 1 + low)),
            )

        return send

    q2, q3 = lax.switch(turn[0], [meet(t) for t in range(2 * nl)], second, third)

    payload = jax.ShapeDtypeStruct(((5 * stride + 1) // 2, SUB, width), f32)
    turned, to_east, to_west = pl.pallas_call(
        functools.partial(turn_fields, levels, rows),
        in_specs=[smem] + [vmem] * 11,
        out_specs=[vmem] * 3,
        out_shape=[jax.ShapeDtypeStruct((5, stride, PADDED, LANES), f32), payload, payload],
        scratch_shapes=[
            pltpu.VMEM((5, length, width), f32),
            pltpu.VMEM((half + 1, SUB, width), f32),
            pltpu.VMEM((SUB, width), f32),
        ],
        compiler_params=params(20),
    )(seam, *fields, indicator, total, second, third, q1, q2, q3)
    from_west = lax.ppermute(to_east, "lon", [(i, (i + 1) % nl) for i in range(nl)])
    from_east = lax.ppermute(to_west, "lon", [((i + 1) % nl, i) for i in range(nl)])

    nc = width // SUB
    column = jax.ShapeDtypeStruct((nc + 1, stride, SUB, LANES), f32)
    single = jax.ShapeDtypeStruct((nc + 1, SUB, LANES), f32)
    inner = pl.pallas_call(
        functools.partial(inner_step, levels, rows),
        in_specs=[vmem],
        out_specs=[vmem] * 21,
        out_shape=[column] * 19 + [single] * 2,
        scratch_shapes=[pltpu.VMEM((stride, SUB, LANES), f32)] * 2,
        compiler_params=params(24),
        cost_estimate=pl.CostEstimate(flops=20_000_000, bytes_accessed=10_000_000, transcendentals=0),
    )(turned)
    return pl.pallas_call(
        functools.partial(outer_step, levels, rows),
        in_specs=[vmem] * 24,
        out_specs=[anywhere] * 2,
        out_shape=[jax.ShapeDtypeStruct(temp.shape, f32)] * 2,
        scratch_shapes=[pltpu.VMEM((2 * HALO, stride, SUB, LANES), f32)] * 17
        + [pltpu.VMEM((2 * HALO, SUB, LANES), f32)] * 2
        + [
            pltpu.VMEM((2, stride, PADDED, LANES), f32),
            pltpu.VMEM((2, length, width), f32),
            pltpu.VMEM((2, levels, rows, width), f32),
            pltpu.SemaphoreType.DMA((2 * levels,)),
        ],
        compiler_params=params(32),
    )(turned, from_east, from_west, *inner)


def solution(mesh):
    in_specs = (
        P(None, "lat", "lon"),
        P(None, "lat", "lon"),
        P(None, "lat", "lon"),
        P(None, "lat", "lon"),
        P("lat", "lon"),
        P("lat", "lon"),
        P(),
    )
    out_specs = (P(None, "lat", "lon"), P(None, "lat", "lon"))
    body = functools.partial(local, mesh.shape["lon"], mesh.shape["lat"])
    return jax.shard_map(body, mesh=mesh, in_specs=in_specs, out_specs=out_specs, check_vma=False)
```

```python
import functools

import jax
import jax.numpy as jnp
from jax import lax
from jax.experimental import pallas as pl
from jax.experimental.pallas import tpu as pltpu
from jax.sharding import PartitionSpec as P

RATIO_FLOOR = 0.05
DIFFUSIVITY = 0.1
THERMAL_COEF = 0.2
HALINE_COEF = 0.8

BATCH = 3
STEPS = 1
HALO = 4
SUB = 8
LANES = 128
PADDED = LANES + LANES // SUB


def sublanes():
    return lax.broadcasted_iota(jnp.int32, (SUB, LANES), 0)


def lanes():
    return lax.broadcasted_iota(jnp.int32, (SUB, LANES), 1)


def half_turn(tile):
    return pltpu.roll(tile, 4, 0)


def as_mask(flag):
    return (jnp.zeros((SUB, LANES), jnp.int32) + flag) > 0


def wet_count(indicator, total):
    return jnp.where(indicator == 1, total, 0).astype(jnp.float32)


def fold_half(seam):
    return (2 * (seam[0] & (LANES - 1)) < LANES).astype(jnp.int32)


def pack_rows(levels, width, seam, *refs):
    south, north, (ind_s, ind_n, tot_s, tot_n), (first, second, third, turn) = refs[:4], refs[4:8], refs[8:12], refs[12:]
    low_half = fold_half(seam)
    turn[0] = 2 * lax.div(seam[0], width) + low_half
    lat = lax.axis_index("lat")
    odd = as_mask(lat % 2)
    upper = sublanes() >= HALO
    for i in range(2 * levels):
        f, k = divmod(i, levels)
        low = jnp.where(upper, half_turn(south[f + 2][k]), south[f][k])
        high = jnp.where(upper, north[f][k], half_turn(north[f + 2][k]))
        first[i] = jnp.where(odd, low, high)
        second[i] = jnp.where(odd, high, low)
    low = wet_count(ind_s[...], tot_s[...])
    high = wet_count(ind_n[...], tot_n[...])
    first[2 * levels] = jnp.where(odd, low, high)
    second[2 * levels] = jnp.where(odd, high, low)

    for i in range(levels + 1):
        third[i] = jnp.zeros((SUB, LANES), jnp.float32)

    @pl.when(lat == lax.axis_size("lat") - 1)
    def _():
        for i in range(2 * levels):
            f, k = divmod(i, levels)
            for j in range(HALO):
                second[i, j : j + 1, :] = north[f][k, 7 - j : 8 - j, :]
                row = 7 - j if f == 0 else (6, 5, 4, 7)[j]
                second[i, HALO + j : HALO + j + 1, :] = -north[f + 2][k, row : row + 1, :]
        for j in range(HALO):
            second[2 * levels, j : j + 1, :] = wet_count(ind_n[7 - j : 8 - j, :], tot_n[7 - j : 8 - j, :])
        low = as_mask(low_half)
        for i in range(levels + 1):
            even = second[2 * i]
            odd_one = second[min(2 * i + 1, 2 * levels)]
            left = jnp.where(low, even, pltpu.roll(even, LANES // 2, 1))
            right = jnp.where(low, pltpu.roll(odd_one, LANES // 2, 1), odd_one)
            third[i] = jnp.where(lanes() < LANES // 2, left, right)


def stretch(levels, rows):
    blocks = LANES // levels
    stride = -(-(rows + 2 * HALO) // blocks)
    return blocks, stride, blocks * stride, -(-(HALO + stride * (LANES + 1)) // SUB) * SUB


def turn_fields(levels, rows, seam, *refs):
    fields, ind, tot, block, half_block, q1, q2, q3, turned, to_east, to_west, flat, north_halo, spare = refs[:4], *refs[4:]
    blocks, stride, period, length = stretch(levels, rows)
    half = 2 * levels
    nl = lax.axis_size("lon")
    lat = lax.axis_index("lat")
    odd = as_mask(lat % 2)
    closed = as_mask((lat == 0).astype(jnp.int32))
    lane = lanes()
    upper = sublanes() >= HALO

    def south_halo(i):
        return jnp.where(closed, 0.0, jnp.where(odd, q1[i], q2[i]))

    for i in range(half + 1):
        north_halo[i] = jnp.where(odd, q2[i], q1[i])

    @pl.when(lat == lax.axis_size("lat") - 1)
    def _():
        r = seam[0] & (LANES - 1)
        low = fold_half(seam)
        home = lax.div(seam[0], LANES) - 2 * lax.axis_index("lon") + 2 * nl
        whole_own = as_mask((lax.rem(home - low, nl) == 0).astype(jnp.int32))
        half_own = as_mask((lax.rem(home - 1 + low, nl) == 0).astype(jnp.int32))
        for i in range(half + 1):
            at = r - lane - jnp.where(upper, 1 if i < levels else 0, 0)

            def pick(tile, column):
                return jnp.take_along_axis(tile, column & (LANES - 1), axis=1, mode="promise_in_bounds")

            whole = pick(jnp.where(whole_own, block[i], q2[i]), at)
            offset = LANES // 2 * (1 - low + i % 2)
            part = pick(jnp.where(half_own, half_block[i // 2], q3[i // 2]), at + offset)
            north_halo[i] = jnp.where((1 - 2 * low) * at >= low, whole, part)

    def turn(f):
        end = levels * period
        for t in range(end // SUB * SUB, length, SUB):
            keep = sublanes() + t < end
            flat[f, t : t + SUB, :] = jnp.where(keep, flat[f, t : t + SUB, :], 0.0)
        for t in range(stride):
            turned[f, t, 0:LANES, :] = flat.at[f][pl.ds(HALO + t, LANES, stride=stride), :].T

    tiles = rows // SUB
    for f in range(4):

        def fill(k, carry):
            at = HALO + HALO + k * period
            for t in range(tiles):
                flat[f, pl.ds(at + t * SUB, SUB), :] = fields[f][k, t * SUB : t * SUB + SUB, :]
            i = (f % 2) * levels + k
            n_tile, s_tile = north_halo[i], south_halo(i)
            if f >= 2:
                n_tile, s_tile = half_turn(n_tile), half_turn(s_tile)
            flat[f, pl.ds(at - SUB, SUB), :] = jnp.where(upper, s_tile, 0.0)
            flat[f, pl.ds(at + rows, SUB), :] = jnp.where(upper, 0.0, n_tile)
            return carry

        lax.fori_loop(0, levels, fill, 0, unroll=12)
        turn(f)
    for t in range(tiles + 2):
        if t == 0:
            n = jnp.where(upper, south_halo(half), 0.0)
        elif t == tiles + 1:
            n = jnp.where(upper, 0.0, north_halo[half])
        else:
            n = wet_count(ind[t * SUB - SUB : t * SUB, :], tot[t * SUB - SUB : t * SUB, :])

        def left_over(k, carry):
            flat[4, pl.ds(HALO + HALO + k * period + (t - 1) * SUB, SUB), :] = n - k.astype(jnp.float32)
            return carry

        lax.fori_loop(0, levels, left_over, 0, unroll=12)

    turn(4)

    west = east = jnp.zeros((SUB, LANES), jnp.float32)
    for t in range(stride):
        here = (lane >= blocks * t) & (lane < blocks * (t + 1))
        west = jnp.where(here, pltpu.roll(turned[4, t, 0:SUB, :], blocks * t, 1), west)
        east = jnp.where(here, pltpu.roll(turned[4, t, LANES - SUB : LANES, :], blocks * t, 1), east)
    places = [(f, t) for f in range(4) for t in range(stride)]
    first = (len(places) + 1) // 2
    to_west[first], to_east[first] = west, east
    for i in range(first):
        f, t = places[i]
        west, east = turned[f, t, 0:SUB, :], turned[f, t, LANES - SUB : LANES, :]
        if i + first < len(places):
            f, t = places[i + first]
            west = jnp.where(upper, half_turn(turned[f, t, 0:SUB, :]), west)
            east = jnp.where(upper, east, half_turn(turned[f, t, LANES - SUB : LANES, :]))
        to_west[i] = west
        to_east[i] = east


def ahead(tiles):
    return tiles[1:] + [pltpu.roll(tiles[0], LANES - 1, 1)]


def behind(tiles):
    return [pltpu.roll(tiles[-1], 1, 1)] + tiles[:-1]


def each(function, *lists):
    return [function(*items) for items in zip(*lists)]


def pairs(function, *lists):
    return tuple(map(list, zip(*each(function, *lists))))


def replaced(tiles, other):
    return [other.get(t, x) for t, x in enumerate(tiles)]


def flux_pair(q, q_next, half_speed, half_size):
    anti = half_size * (q_next - q)
    return half_speed * (q_next + q) - anti, anti


def limited_flux(anti, plus, minus, plus_next, minus_next):
    return anti * jnp.where(anti >= 0.0, jnp.minimum(plus_next, minus), jnp.minimum(plus, minus_next))


def reciprocal(x):
    return pl.reciprocal(x, approx=True)


def halves(speed, mask):
    half = jnp.where(mask > 0.0, 0.5 * speed, 0.0)
    return half, jnp.abs(half)


def net(q, a, b, c, d):
    return q - ((a - b) + (c - d))


def ratios(a, b, c, l, sa, sb, sc, sl):
    inflow = (jnp.maximum(b, 0.0) - jnp.minimum(a, 0.0)) + (jnp.maximum(l, 0.0) - jnp.minimum(c, 0.0))
    outflow = (jnp.maximum(a, 0.0) - jnp.minimum(b, 0.0)) + (jnp.maximum(c, 0.0) - jnp.minimum(l, 0.0))
    rise = jnp.maximum(jnp.maximum(jnp.maximum(sa, sc), 0.0), -jnp.minimum(sb, sl))
    drop = jnp.maximum(jnp.maximum(jnp.maximum(sb, sl), 0.0), -jnp.minimum(sa, sc))
    plus = jnp.minimum(1.0, rise * reciprocal(jnp.maximum(inflow, RATIO_FLOOR)))
    minus = jnp.minimum(1.0, drop * reciprocal(jnp.maximum(outflow, RATIO_FLOOR)))
    return plus, minus


def face(t0, t1, s0, s1, zt0, zt1, zs0, zs1, m):
    dt, ds, zt, zs = t1 - t0, s1 - s0, zt1 + zt0, zs1 + zs0
    bottom = jnp.maximum(HALINE_COEF * zs - THERMAL_COEF * zt, 1.0)
    half_slope = (HALINE_COEF * ds - THERMAL_COEF * dt) * reciprocal(bottom)
    half_slope = jnp.maximum(jnp.minimum(half_slope, 1.0), -1.0)
    return jnp.where(m > 0.0, dt - half_slope * zt, 0.0), jnp.where(m > 0.0, ds - half_slope * zs, 0.0)


class Phases:
    def __init__(self, levels, rows, cell, read, write, alt_read, alt_write):
        blocks, stride, period, length = stretch(levels, rows)
        self.blocks, self.ts, self.nc = blocks, range(stride), LANES // SUB
        self.cell, self.read, self.write = cell, read, write
        self.alt_read, self.alt_write = alt_read, alt_write
        self.held = {}
        self.seam = (rows + HALO - 1) % stride
        self.spare = (rows + 2 * HALO - 1) % stride
        on_top = lax.axis_index("lat") == lax.axis_size("lat") - 1
        tops = as_mask(on_top.astype(jnp.int32))
        self.at_seam = (lanes() % blocks == (rows + HALO - 1) // stride) & tops
        self.first_row, self.last_row = sublanes() == 0, sublanes() == SUB - 1

    def fixed(self, c):
        return c[1] if isinstance(c[0], int) else None

    def load(self, key, c):
        if (key, c[1]) not in self.held:
            fetch = self.cell if isinstance(key, str) else self.read
            self.held[key, c[1]] = [fetch(key, c, t) for t in self.ts]
        return self.held[key, c[1]]

    def following(self, key, c):
        i, nc = self.fixed(c), self.nc
        if i not in (nc - 1, nc):
            return self.load(key, (c[0], c[1] + 1))
        if (key, "next", i) not in self.held:
            own, halo = self.load(key, (0, 0)), self.load(key, (0, nc))
            one, other = (halo, own) if i == nc - 1 else (own, halo)
            self.held[key, "next", i] = [
                pltpu.roll(jnp.where(self.first_row, x, y), SUB - 1, 0) for x, y in zip(one, other)
            ]
        return self.held[key, "next", i]

    def mixed(self, i, last, halo):
        one, other = (halo, last) if i == 0 else (last, halo)
        return [pltpu.roll(jnp.where(self.last_row, x, y), 1, 0) for x, y in zip(one, other)]

    def preceding(self, key, c):
        i, nc = self.fixed(c), self.nc
        if i in (0, nc):
            return self.mixed(i, self.load(key, (0, nc - 1)), self.load(key, (0, nc)))
        return self.load(key, (c[0], c[1] - 1))

    def put(self, place, c, tiles):
        for t in self.ts:
            self.write(place, c, t, tiles[t])

    def upwind_face(self, c):
        m = each(jnp.minimum, self.load("m", c), self.following("m", c))
        speed = pairs(halves, self.load("u", c), m)
        parts = [pairs(flux_pair, self.load(f, c), self.following(f, c), *speed) for f in "TS"]
        self.put(15, c, m)
        for f in range(2):
            self.put(4 + f, c, parts[f][1])
        return [low for low, _ in parts]

    def upwind_cell(self, c, here, before):
        s = self.seam
        m, v = self.load("m", c), self.load("v", c)
        open_a = each(jnp.minimum, m, ahead(m))
        speed = pairs(halves, v, open_a)
        alt = halves(jnp.where(self.at_seam, v[self.spare], v[s]), open_a[s])
        results = []
        for f, key in enumerate("TS"):
            q = self.load(key, c)
            q_a = ahead(q)
            low_a, anti_a = pairs(flux_pair, q, q_a, *speed)
            low_alt, anti_alt = flux_pair(q[s], q_a[s], *alt)
            low_b = behind(replaced(low_a, {s: low_alt}))
            results.append((each(net, q, low_a, low_b, here[f], before[f]), anti_a, anti_alt))
        self.put(14, c, open_a)
        self.put(16, c, m)
        for f, (upwind, anti_a, anti_alt) in enumerate(results):
            self.put(f, c, upwind)
            self.put(2 + f, c, anti_a)
            self.alt_write(f, c, anti_alt)

    def ratio_face(self, c):
        m = self.load(15, c)
        return [
            each(lambda x, n, o: jnp.where(o > 0.0, n - x, 0.0), self.load(f, c), self.following(f, c), m)
            for f in range(2)
        ]

    def ratio_cell(self, c, here, before):
        open_a = self.load(14, c)
        results = []
        for f in range(2):
            up, anti_a = self.load(f, c), self.load(2 + f, c)
            step_a = each(lambda x, n, o: jnp.where(o > 0.0, n - x, 0.0), up, ahead(up), open_a)
            anti_b = behind(replaced(anti_a, {self.seam: self.alt_read(f, c)}))
            anti_c, anti_l = self.load(4 + f, c), self.preceding(4 + f, c)
            results.append(
                pairs(ratios, anti_a, anti_b, anti_c, anti_l, step_a, behind(step_a), here[f], before[f])
            )
        for f, (plus, minus) in enumerate(results):
            self.put(6 + f, c, plus)
            self.put(8 + f, c, minus)

    def limited_face(self, c):
        return [
            each(
                limited_flux, self.load(4 + f, c), self.load(6 + f, c), self.load(8 + f, c),
                self.following(6 + f, c), self.following(8 + f, c),
            )
            for f in range(2)
        ]

    def limited_cell(self, c, here, before):
        s, m = self.seam, self.load(16, c)
        results = []
        for f in range(2):
            plus, minus = self.load(6 + f, c), self.load(8 + f, c)
            plus_a, minus_a = ahead(plus), ahead(minus)
            lim_a = each(limited_flux, self.load(2 + f, c), plus, minus, plus_a, minus_a)
            lim_alt = limited_flux(self.alt_read(f, c), plus[s], minus[s], plus_a[s], minus_a[s])
            lim_b = behind(replaced(lim_a, {s: lim_alt}))
            new = each(net, self.load(f, c), lim_a, lim_b, here[f], before[f])
            results.append(
                (new, each(lambda x, n: jnp.where(n > 1.0, pltpu.roll(x, LANES - self.blocks, 1) - x, 0.0), new, m))
            )
        for f, (new, below) in enumerate(results):
            self.put(10 + f, c, new)
            self.put(12 + f, c, below)

    def diffuse_face(self, c):
        sides = [side for p in (10, 11, 12, 13) for side in (self.load(p, c), self.following(p, c))]
        return list(pairs(face, *sides, self.load(15, c)))

    def diffuse_cell(self, c, here, before):
        values = [self.load(p, c) for p in (10, 11, 12, 13)]
        along = pairs(face, *[side for x in values for side in (x, ahead(x))], self.load(14, c))
        for f in range(2):
            new = each(
                lambda q, a, b, x, y: q + DIFFUSIVITY * ((a - b) + (x - y)),
                values[f], along[f], behind(along[f]), here[f], before[f],
            )
            self.put(17 + f, c, new)

    def all(self):
        return (
            (self.upwind_face, self.upwind_cell),
            (self.ratio_face, self.ratio_cell),
            (self.limited_face, self.limited_cell),
            (self.diffuse_face, self.diffuse_cell),
        )


FIELDS = "TSuvm"


def inner_step(levels, rows, turned, *refs):
    grid, alts, prev = refs[:19], refs[19:21], refs[21:]

    def cell(key, c, t):
        return turned.at[FIELDS.index(key), t][pl.ds(sum(c), SUB, stride=LANES // SUB), :]

    def read(place, c, t):
        return grid[place][sum(c), t]

    def write(place, c, t, tile):
        grid[place][sum(c), t] = tile

    def alt_read(f, c):
        return alts[f][sum(c)]

    def alt_write(f, c, tile):
        alts[f][sum(c)] = tile

    phases = Phases(levels, rows, cell, read, write, alt_read, alt_write)
    ts = phases.ts

    def store(lists):
        for ref, tiles in zip(prev, lists):
            for t in ts:
                ref[t] = tiles[t]

    for i, (make_face, make_cell) in enumerate(phases.all()):
        low, high = i + 1, phases.nc - 1 - i
        count = (high - low) // STEPS
        phases.held.clear()
        store(make_face((0, low - 1)))

        def some(g, carry):
            start = low + g * count
            phases.held.clear()
            before = [[ref[t] for t in ts] for ref in prev]
            for n in range(count):
                here = make_face((start, n))
                make_cell((start, n), here, before)
                before = here
            store(before)
            phases.held.clear()
            return carry

        lax.fori_loop(0, STEPS, some, 0)


def outer_step(levels, rows, turned, from_east, from_west, *refs):
    inner, inner_alts, (temp_out, salt_out), refs = refs[:19], refs[19:21], refs[21:23], refs[23:]
    grid, alts, result, flat, out, sems = refs[:17], refs[17:19], *refs[19:]
    blocks, stride, period, length = stretch(levels, rows)
    ts = range(stride)
    upper = sublanes() >= HALO
    first = (4 * stride + 1) // 2
    nc = LANES // SUB
    lane = lanes()
    halo_count = jnp.where(upper, from_west[first], from_east[first])
    made = [set() for _ in range(17)]
    made_alts = set()

    def slot(c):
        return (sum(c) + HALO) % (nc + 1)

    def cell(key, c, t):
        f = FIELDS.index(key)
        if sum(c) < nc:
            return turned.at[f, t][pl.ds(sum(c), SUB, stride=nc), :]
        if f == 4:
            index = blocks * t + lane % blocks
            n = jnp.take_along_axis(halo_count, index, axis=1, mode="promise_in_bounds")
            return n - lax.div(lane, blocks).astype(jnp.float32)
        i = f * stride + t
        if i < first:
            return jnp.where(upper, from_west[i], from_east[i])
        return half_turn(jnp.where(upper, from_east[i - first], from_west[i - first]))

    def read(place, c, t):
        return grid[place][slot(c), t] if sum(c) in made[place] else inner[place][sum(c), t]

    def write(place, c, t, tile):
        if place < 17:
            made[place].add(sum(c))
            grid[place][slot(c), t] = tile
        elif sum(c) < nc:
            result.at[place - 17, t][pl.ds(sum(c), SUB, stride=nc), :] = tile

    def alt_read(f, c):
        return alts[f][slot(c)] if sum(c) in made_alts else inner_alts[f][sum(c)]

    def alt_write(f, c, tile):
        made_alts.add(sum(c))
        alts[f][slot(c)] = tile

    phases = Phases(levels, rows, cell, read, write, alt_read, alt_write)
    for i, (make_face, make_cell) in enumerate(phases.all()):
        columns = [*range(nc - 1 - i, nc + 1), *range(i + 1)]
        phases.held.clear()
        faces = {c: make_face((0, c)) for c in [columns[0] - 1] + columns}
        for c in columns:
            if c == nc and i == 3:
                continue
            if c in (0, nc):
                before = each(lambda x, h: phases.mixed(c, x, h), faces[nc - 1], faces[nc])
            else:
                before = faces[c - 1]
            make_cell((0, c), faces[c], before)
    for f in range(2):
        for c in range(4, nc - 4):
            for t in ts:
                result.at[f, t][pl.ds(c, SUB, stride=nc), :] = inner[17 + f][c, t]

    stores = []
    for f, ref in enumerate((temp_out, salt_out)):
        for t in ts:
            flat.at[f][pl.ds(HALO + t, LANES, stride=stride), :] = result[f, t, 0:LANES, :].T
        for g in range(0, levels, BATCH):
            for k in range(g, g + BATCH):
                for t in range(rows // SUB):
                    at = HALO + HALO + k * period + t * SUB
                    out[f, k, t * SUB : t * SUB + SUB, :] = flat[f, at : at + SUB, :]
            levels_of = pl.ds(g, BATCH)
            store = pltpu.make_async_copy(out.at[f, levels_of], ref.at[levels_of], sems.at[len(stores)])
            store.start()
            stores.append(store)
    for store in stores:
        store.wait()


def local(nl, nlat, temp, salt, east, north, indicator, total, seam):
    levels, rows, width = temp.shape
    half = 2 * levels
    blocks, stride, period, length = stretch(levels, rows)
    vmem = pl.BlockSpec(memory_space=pltpu.VMEM)
    smem = pl.BlockSpec(memory_space=pltpu.SMEM)
    anywhere = pl.BlockSpec(memory_space=pl.ANY)
    f32 = jnp.float32

    def params(mib):
        return pltpu.CompilerParams(vmem_limit_bytes=mib * 1024 * 1024)

    last = rows // SUB - 1
    low = pl.BlockSpec((levels, SUB, width), lambda i: (0, 0, 0))
    high = pl.BlockSpec((levels, SUB, width), lambda i: (0, last, 0))
    flat_low = pl.BlockSpec((SUB, width), lambda i: (0, 0))
    flat_high = pl.BlockSpec((SUB, width), lambda i: (last, 0))
    block = jax.ShapeDtypeStruct((half + 1, SUB, width), f32)
    whole_block = pl.BlockSpec((half + 1, SUB, width), lambda i: (0, 0, 0))
    fields = (temp, salt, east, north)
    halves_block = jax.ShapeDtypeStruct((levels + 1, SUB, width), f32)
    whole_halves = pl.BlockSpec((levels + 1, SUB, width), lambda i: (0, 0, 0))
    first, second, third, turn = pl.pallas_call(
        functools.partial(pack_rows, levels, width),
        grid=(1,),
        in_specs=[smem] + [low] * 4 + [high] * 4 + [flat_low, flat_high] * 2,
        out_specs=[whole_block] * 2 + [whole_halves, smem],
        out_shape=[block] * 2 + [halves_block, jax.ShapeDtypeStruct((1,), jnp.int32)],
        compiler_params=params(56),
    )(seam, *fields, *fields, indicator, indicator, total, total)

    q1 = lax.ppermute(first, "lat", [(j, j ^ 1) for j in range(nlat)])

    def meet(index):
        back, low = divmod(index, 2)

        def facing(back):
            pairs = []
            for i in range(nl):
                to = (back - i) % nl
                to = (i + nl // 2) % nl if to == i else to
                pairs.append((i * nlat + nlat - 1, to * nlat + nlat - 1))
            return pairs

        def idle(rows):
            return [(i * nlat + j, (i ^ 1) * nlat + j) for i in range(nl) for j in rows]

        inner = [(i * nlat + j, i * nlat + (j + 1 if j % 2 else j - 1)) for i in range(nl) for j in range(1, nlat - 1)]

        def send(x, y):
            return (
                lax.ppermute(x, ("lon", "lat"), idle([0]) + inner + facing(back - low)),
                lax.ppermute(y, ("lon", "lat"), idle(range(nlat - 1)) + facing(back - 1 + low)),
            )

        return send

    q2, q3 = lax.switch(turn[0], [meet(t) for t in range(2 * nl)], second, third)

    payload = jax.ShapeDtypeStruct(((4 * stride + 1) // 2 + 1, SUB, width), f32)
    turned, to_east, to_west = pl.pallas_call(
        functools.partial(turn_fields, levels, rows),
        in_specs=[smem] + [vmem] * 11,
        out_specs=[vmem] * 3,
        out_shape=[jax.ShapeDtypeStruct((5, stride, PADDED, LANES), f32), payload, payload],
        scratch_shapes=[
            pltpu.VMEM((5, length, width), f32),
            pltpu.VMEM((half + 1, SUB, width), f32),
            pltpu.VMEM((SUB, width), f32),
        ],
        compiler_params=params(20),
    )(seam, *fields, indicator, total, second, third, q1, q2, q3)
    from_west = lax.ppermute(to_east, "lon", [(i, (i + 1) % nl) for i in range(nl)])
    from_east = lax.ppermute(to_west, "lon", [((i + 1) % nl, i) for i in range(nl)])

    nc = width // SUB
    column = jax.ShapeDtypeStruct((nc + 1, stride, SUB, LANES), f32)
    single = jax.ShapeDtypeStruct((nc + 1, SUB, LANES), f32)
    inner = pl.pallas_call(
        functools.partial(inner_step, levels, rows),
        in_specs=[vmem],
        out_specs=[vmem] * 21,
        out_shape=[column] * 19 + [single] * 2,
        scratch_shapes=[pltpu.VMEM((stride, SUB, LANES), f32)] * 2,
        compiler_params=params(24),
        cost_estimate=pl.CostEstimate(flops=20_000_000, bytes_accessed=10_000_000, transcendentals=0),
    )(turned)
    return pl.pallas_call(
        functools.partial(outer_step, levels, rows),
        in_specs=[vmem] * 24,
        out_specs=[anywhere] * 2,
        out_shape=[jax.ShapeDtypeStruct(temp.shape, f32)] * 2,
        scratch_shapes=[pltpu.VMEM((2 * HALO, stride, SUB, LANES), f32)] * 17
        + [pltpu.VMEM((2 * HALO, SUB, LANES), f32)] * 2
        + [
            pltpu.VMEM((2, stride, PADDED, LANES), f32),
            pltpu.VMEM((2, length, width), f32),
            pltpu.VMEM((2, levels, rows, width), f32),
            pltpu.SemaphoreType.DMA((2 * levels,)),
        ],
        compiler_params=params(32),
    )(turned, from_east, from_west, *inner)


def solution(mesh):
    in_specs = (
        P(None, "lat", "lon"),
        P(None, "lat", "lon"),
        P(None, "lat", "lon"),
        P(None, "lat", "lon"),
        P("lat", "lon"),
        P("lat", "lon"),
        P(),
    )
    out_specs = (P(None, "lat", "lon"), P(None, "lat", "lon"))
    body = functools.partial(local, mesh.shape["lon"], mesh.shape["lat"])
    return jax.shard_map(body, mesh=mesh, in_specs=in_specs, out_specs=out_specs, check_vma=False)
```
